512 devices in a mesh: sample: 32 (over x_lo, y, core), head: 16 (over z, x_hi).
Axes of the slice: x: 4 (x_hi: 2, x_lo: 2; x = x_hi * 2 + x_lo), y: 8, z: 8, core: 2. Of those that a mesh axis runs over, the one named last changes fastest.
Arguments:
- q_nope: bfloat16 [4096, 8192], P('sample', 'head'), may hold values from -6 to 6
- q_rope: bfloat16 [4096, 4096], P('sample', 'head'), may hold values from -12 to 12
- resp_latent: bfloat16 [4096, 512], P('sample'), may hold values from -6 to 6
- resp_rope_t: bfloat16 [64, 4096], P(None, 'sample'), may hold values from -6 to 6
- prompt_latent: bfloat16 [512, 512], P('sample'), may hold values from -6 to 6
- prompt_rope_t: bfloat16 [64, 512], P(None, 'sample'), may hold values from -4 to 4
- w_key_up: bfloat16 [512, 8192], P(None, 'head'), may hold values from -0.5 to 0.5
- w_value_up: bfloat16 [512, 8192], P(None, 'head'), may hold values from -0.25 to 0.25
- grad_out: bfloat16 [4096, 8192], P('sample', 'head'), may hold values from -6 to 6
- lengths: int32 [32], P('sample'), may hold values from 1 to 128, as said below
Outputs:
- d_q_nope: bfloat16 [4096, 8192], P('sample', 'head')
- d_q_rope: bfloat16 [4096, 4096], P('sample', 'head')
- d_key_up: float32 [512, 8192], P('sample', 'head')
- d_value_up: float32 [512, 8192], P('sample', 'head')
- d_prompt_latent: float32 [512, 512], P('sample')
- d_prompt_rope_t: float32 [64, 512], P(None, 'sample')
- d_resp_latent: float32 [4096, 512], P('sample')
- d_resp_rope_t: float32 [64, 4096], P(None, 'sample')
The draws below stay inside these ranges and needn't reach their ends.
Inputs may be any that keep to these rules, and one draw needn't show every extreme that they name: `lengths`: some rollout has length exactly 128.
All inputs are finite; a program needn't handle non-finite values.
Results may differ from the reference program's by a relative error of at most 0.03.
Values may be sent and summed in bfloat16 or wider, within the bound.
No kernel may reach another device: no remote copies, remote signals or barrier semaphores. Data moves between devices by JAX's collectives and lax.ppermute only.
A program may use at most 64 MiB of HBM per device.

```python
import jax
import jax.numpy as jnp
from jax import lax

DC = 512
DR = 64
DN = 128
DV = 128
RESP = 128
HEADS = 64
ROLLOUTS = 32
TOKENS = 4096
PROMPT = 512


def rope_base(key):
    return jax.random.normal(key, (DR, PROMPT), jnp.float32)


def draw_prompt_rope_t(key, part):
    shared = rope_base(key)
    return jnp.clip(shared, -4.0, 4.0).astype(jnp.bfloat16)


def draw_q_rope(key, part):
    key = jax.random.fold_in(key, 12)
    normal_part = jnp.clip(jax.random.normal(key, (TOKENS, HEADS, DR), jnp.float32), -4.0, 4.0)
    return normal_part.reshape(TOKENS, HEADS * DR).astype(jnp.bfloat16)


def draw_lengths(key, part):
    key = jax.random.fold_in(key, 13)
    first_key, second_key = jax.random.split(key)
    drawn_lengths = jax.random.randint(first_key, (ROLLOUTS,), 1, RESP + 1)
    longest = jax.random.randint(second_key, (), 0, ROLLOUTS)
    return jnp.where(jnp.arange(ROLLOUTS) == longest, RESP, drawn_lengths).astype(jnp.int32)


def levels(stream_key, extent, cuts, least, top_value):
    level = 1.0
    for axis_at, parts in cuts:
        draws = jax.random.uniform(jax.random.fold_in(jax.random.fold_in(stream_key, 6), axis_at), (parts,), jnp.float32, least / len(cuts), top_value / len(cuts))
        level = level * jnp.repeat(jnp.exp(draws), extent[axis_at] // parts).reshape((-1,) + (1,) * (len(extent) - 1 - axis_at))
    return level


def bell_draw(rng, shape, deviation, bound, cuts=(), kind=jnp.bfloat16):
    values = jax.random.normal(rng, shape, jnp.float32) * deviation
    if len(cuts) > 0:
        values = levels(rng, shape, cuts, -0.22, 0.18) * values
    return jnp.clip(values, min=-bound, max=bound).astype(kind)


def setup_inputs(seed: int = 0) -> dict:
    streams_of = jax.random.split(jax.random.key(seed), 11)
    return {
        "q_nope": bell_draw(streams_of[0], (TOKENS, HEADS * DN), 1.0, 6.0, ((0, 32), (1, 16))),
        "q_rope": draw_q_rope(jax.random.fold_in(streams_of[10], 71), 0),
        "resp_latent": bell_draw(streams_of[2], (TOKENS, DC), 1.0, 6.0, ((0, 32),)),
        "resp_rope_t": bell_draw(streams_of[3], (DR, TOKENS), 1.0, 6.0, ((1, 32),)),
        "prompt_latent": bell_draw(streams_of[4], (PROMPT, DC), 1.0, 6.0, ((0, 32),)),
        "prompt_rope_t": draw_prompt_rope_t(jax.random.fold_in(streams_of[10], 71), 0),
        "w_key_up": bell_draw(streams_of[6], (DC, HEADS * DN), DN ** -0.5, 0.5, ((1, 16),)),
        "w_value_up": bell_draw(streams_of[7], (DC, HEADS * DV), DC ** -0.5, 0.25, ((1, 16),)),
        "grad_out": bell_draw(streams_of[8], (TOKENS, HEADS * DV), 1.0, 6.0, ((0, 32), (1, 16))),
        "lengths": draw_lengths(jax.random.fold_in(streams_of[10], 71), 0),
    }


def local_grads(query_nope, query_rope, keys_latent, keys_rope, length, grad_rows, w_key_up, w_value_up):
    wide = jnp.float32
    token_rows = query_nope.shape[0]
    head_count = w_key_up.shape[1] // DN
    latent_dim = w_key_up.shape[0]
    prompt_rows = keys_latent.shape[0] - token_rows
    softmax_scale = (DN + DR) ** -0.5
    position = jnp.arange(token_rows, dtype=jnp.int32)
    key_index = jnp.arange(keys_latent.shape[0], dtype=jnp.int32) - prompt_rows
    allowed = (key_index[None, :] < 0) | ((key_index[None, :] <= position[:, None]) & (key_index[None, :] < length))
    live = position < length
    masked_grad = jnp.where(live[:, None], grad_rows, jnp.zeros_like(grad_rows))
    nope_heads = query_nope.reshape(token_rows, head_count, DN).astype(wide)
    rope_heads = query_rope.reshape(token_rows, head_count, DR).astype(wide)
    grad_heads = masked_grad.reshape(token_rows, head_count, DV).astype(wide)
    key_up = w_key_up.reshape(latent_dim, head_count, DN).astype(wide)
    value_up = w_value_up.reshape(latent_dim, head_count, DV).astype(wide)
    latent_keys = keys_latent.astype(wide)
    rope_keys = keys_rope.astype(wide)
    q_latent = jnp.einsum("thn,chn->htc", nope_heads, key_up).astype(jnp.bfloat16)
    scores = jnp.einsum("htc,kc->htk", q_latent.astype(wide), latent_keys) + jnp.einsum("thr,rk->htk", rope_heads, rope_keys)
    scores = jnp.where(allowed[None], softmax_scale * scores, jnp.float32(-1e30))
    highest = jnp.max(scores, axis=-1, keepdims=True)
    exponent = jnp.exp(scores - highest)
    attention = exponent / jnp.sum(exponent, axis=-1, keepdims=True)
    attention_b = attention.astype(jnp.bfloat16)
    out_latent = jnp.einsum("htk,kc->htc", attention_b.astype(wide), latent_keys).astype(jnp.bfloat16)
    d_value_up = jnp.einsum("htc,thv->chv", out_latent.astype(wide), grad_heads).reshape(latent_dim, head_count * DV)
    d_out_latent = jnp.einsum("thv,chv->htc", grad_heads, value_up).astype(jnp.bfloat16)
    d_attention = jnp.einsum("htc,kc->htk", d_out_latent.astype(wide), latent_keys)
    row_delta = jnp.sum(attention * d_attention, axis=-1, keepdims=True)
    d_scores = (softmax_scale * attention * (d_attention - row_delta)).astype(jnp.bfloat16)
    d_scores_w = d_scores.astype(wide)
    d_q_latent = jnp.einsum("htk,kc->htc", d_scores_w, latent_keys).astype(jnp.bfloat16)
    d_q_rope = jnp.einsum("htk,rk->thr", d_scores_w, rope_keys).astype(jnp.bfloat16).reshape(token_rows, head_count * DR)
    d_q_nope = jnp.einsum("htc,chn->thn", d_q_latent.astype(wide), key_up).astype(jnp.bfloat16).reshape(token_rows, head_count * DN)
    d_key_up = jnp.einsum("htc,thn->chn", d_q_latent.astype(wide), nope_heads).reshape(latent_dim, head_count * DN)
    key_latent_grad = jnp.einsum("htk,htc->kc", d_scores_w, q_latent.astype(wide)) + jnp.einsum("htk,htc->kc", attention_b.astype(wide), d_out_latent.astype(wide))
    key_rope_grad = jnp.einsum("htk,thr->rk", d_scores_w, rope_heads)
    return d_q_nope, d_q_rope, d_key_up, d_value_up, key_latent_grad, key_rope_grad


def reference(q_nope, q_rope, resp_latent, resp_rope_t, prompt_latent, prompt_rope_t, w_key_up, w_value_up, grad_out, lengths):
    inputs = (
        q_nope.reshape(ROLLOUTS, RESP, HEADS * DN),
        q_rope.reshape(ROLLOUTS, RESP, HEADS * DR),
        resp_latent.reshape(ROLLOUTS, RESP, DC),
        resp_rope_t.reshape(DR, ROLLOUTS, RESP).transpose(1, 0, 2),
        grad_out.reshape(ROLLOUTS, RESP, HEADS * DV),
        lengths,
    )
    start = (
        jnp.zeros((DC, HEADS * DN), jnp.float32),
        jnp.zeros((DC, HEADS * DV), jnp.float32),
        jnp.zeros((PROMPT, DC), jnp.float32),
        jnp.zeros((DR, PROMPT), jnp.float32),
    )

    def rollout(totals, pieces):
        query_nope, query_rope, own_latent, own_rope, grad_rows, length = pieces
        keys_latent = jnp.concatenate([prompt_latent, own_latent], axis=0)
        keys_rope = jnp.concatenate([prompt_rope_t, own_rope], axis=1)
        grads = local_grads(query_nope, query_rope, keys_latent, keys_rope, length, grad_rows, w_key_up, w_value_up)
        new_totals = (
            totals[0] + grads[2],
            totals[1] + grads[3],
            totals[2] + grads[4][:PROMPT],
            totals[3] + grads[5][:, :PROMPT],
        )
        return new_totals, (grads[0], grads[1], grads[4][PROMPT:], grads[5][:, PROMPT:])

    totals, stacked = lax.scan(rollout, start, inputs)
    d_q_nope = stacked[0].reshape(TOKENS, HEADS * DN)
    d_q_rope = stacked[1].reshape(TOKENS, HEADS * DR)
    d_resp_latent = stacked[2].reshape(TOKENS, DC)
    d_resp_rope_t = stacked[3].transpose(1, 0, 2).reshape(DR, TOKENS)
    return (d_q_nope, d_q_rope, totals[0], totals[1], totals[2], totals[3], d_resp_latent, d_resp_rope_t)
```

```python
import jax
import jax.numpy as jnp
from jax import lax
from jax.experimental import pallas as pl
from jax.experimental.pallas import tpu as pltpu
from jax.sharding import Mesh, PartitionSpec as P

DC = 512
DR = 64
DN = 128
DV = 128
RESP = 128
PAGE = 16
LOCAL = 4
ROWS = LOCAL * RESP
EXT = 640
CHIPS = 16
HALF = CHIPS * PAGE
KEYS = 2 * HALF + RESP
WIDE = 2 * LOCAL * DN + EXT
SCALE = (DN + DR) ** (-0.5)
F32 = jnp.float32
BF16 = jnp.bfloat16
SAMPLE = ("xl", "y", "c")
HEAD = ("z", "xh")
PARAMS = pltpu.CompilerParams(vmem_limit_bytes=40 * 1024 * 1024)


def dot(a, b, ca, cb):
    return lax.dot_general(a, b, (((ca,), (cb,)), ((), ())), preferred_element_type=F32)


def columns(part, width):
    return slice(part * width, (part + 1) * width)


def with_rope(latent, rope_t):
    rope = jnp.transpose(rope_t.astype(F32))
    pad = jnp.zeros((latent.shape[0], EXT - DC - DR), F32)
    return jnp.concatenate([latent.astype(F32), rope, pad], axis=1).astype(BF16)


def pages_kernel(latent, rope_t, out):
    page = with_rope(latent[...], rope_t[...])
    for k in range(CHIPS):
        out[k] = page


def main_kernel(
    where,
    q_nope,
    q_rope,
    grad,
    w_key,
    w_value,
    own,
    other,
    resp_latent,
    resp_rope_t,
    d_q_nope,
    d_q_rope,
    send_resp,
    keep,
    send,
    keys,
    query,
    d_out,
    weight,
    prompt,
):
    length = where[0]
    core = where[1]
    keys[0:HALF, :] = own[...].reshape(HALF, EXT)
    keys[HALF : 2 * HALF, :] = other[...].reshape(HALF, EXT)
    keys[2 * HALF : KEYS, :] = with_rope(resp_latent[...], resp_rope_t[...])
    live = lax.broadcasted_iota(jnp.int32, (RESP, LOCAL * DV), 0) < length
    masked = jnp.where(live, grad[...].astype(F32), 0.0).astype(BF16)
    rope_pad = jnp.zeros((RESP, EXT - DC - DR), BF16)
    for h in range(LOCAL):
        rows = columns(h, RESP)
        query[rows, 0:DC] = dot(q_nope[:, columns(h, DN)], w_key[:, columns(h, DN)], 1, 1).astype(
            BF16
        )
        query[rows, DC:EXT] = jnp.concatenate([q_rope[:, columns(h, DR)], rope_pad], axis=1)
        d_out[rows, :] = dot(masked[:, columns(h, DV)], w_value[:, columns(h, DV)], 1, 1).astype(
            BF16
        )
    key_rows = keys[...]
    key_latent = keys[:, 0:DC]
    scores = dot(key_rows, query[...], 1, 1) * SCALE
    token = lax.broadcasted_iota(jnp.int32, (RESP, ROWS), 1) % RESP
    key_at = lax.broadcasted_iota(jnp.int32, (RESP, ROWS), 0)
    allowed = (key_at <= token) & (key_at < length)
    scores = jnp.concatenate(
        [scores[0 : 2 * HALF], jnp.where(allowed, scores[2 * HALF : KEYS], -1e30)], axis=0
    )
    highest = jnp.max(scores, axis=0, keepdims=True)
    exponent = jnp.exp(scores - highest)
    attention = exponent * (1.0 / jnp.sum(exponent, axis=0, keepdims=True))
    attention_b = attention.astype(BF16)
    d_attention = dot(key_latent, d_out[...], 1, 1)
    row_delta = jnp.sum(attention * d_attention, axis=0, keepdims=True)
    d_scores = (SCALE * attention * (d_attention - row_delta)).astype(BF16)
    key_grad = dot(d_scores, query[...], 1, 0)
    key_grad_v = dot(attention_b, d_out[...], 1, 0)
    prompt[:, 0:DC] = (key_grad[:, 0:DC] + key_grad_v).astype(BF16)
    prompt[:, DC:EXT] = key_grad[:, DC:EXT].astype(BF16)
    for g in range(CHIPS):
        at = 2 * HALF + g * 8
        send_resp[g, :, 0:DC] = (key_grad[at : at + 8, 0:DC] + key_grad_v[at : at + 8]).astype(
            BF16
        )
        send_resp[g, :, DC:EXT] = key_grad[at : at + 8, DC:EXT].astype(BF16)
    d_query = dot(key_rows, d_scores, 0, 0).astype(BF16)
    out_latent = dot(key_latent, attention_b, 0, 0).astype(BF16)
    for h in range(LOCAL):
        d_q = d_query[0:DC, columns(h, RESP)]
        d_q_nope[:, columns(h, DN)] = dot(d_q, w_key[:, columns(h, DN)], 0, 0).astype(BF16)
        weight[:, columns(h, DN)] = dot(d_q, q_nope[:, columns(h, DN)], 1, 0).astype(BF16)
        weight[:, columns(LOCAL + h, DN)] = dot(
            out_latent[:, columns(h, RESP)], masked[:, columns(h, DV)], 1, 0
        ).astype(BF16)
    d_rope = jnp.concatenate(
        [
            jnp.transpose(d_query[DC : DC + DR, columns(h, RESP)].astype(F32)) for h in range(LOCAL)
        ],
        axis=1,
    )
    d_q_rope[...] = d_rope.astype(BF16)
    width = 2 * LOCAL * DN
    for k in range(CHIPS):
        mine = pl.ds(pl.multiple_of((2 * k + core) * PAGE, PAGE), PAGE)
        theirs = pl.ds(pl.multiple_of((2 * k + 1 - core) * PAGE, PAGE), PAGE)
        keep[k, :, 0:width] = weight[mine, :]
        send[k, :, 0:width] = weight[theirs, :]
        keep[k, :, width:WIDE] = prompt[k * PAGE : (k + 1) * PAGE, :]
        send[k, :, width:WIDE] = prompt[HALF + k * PAGE : HALF + (k + 1) * PAGE, :]


def middle_kernel(sample_parts, head_parts, d_key_up, d_value_up, out):
    total = sample_parts[0].astype(F32)
    for k in range(1, CHIPS):
        total = total + sample_parts[k].astype(F32)
    d_key_up[...] = total[:, 0 : LOCAL * DN]
    d_value_up[...] = total[:, LOCAL * DN : 2 * LOCAL * DN]
    page = total[:, 2 * LOCAL * DN : WIDE]
    rows = head_parts[0].astype(F32)
    for g in range(1, CHIPS):
        rows = rows + head_parts[g].astype(F32)
    line = jnp.concatenate([rows, page[0:8], page[8:16]], axis=1).astype(BF16)
    for g in range(CHIPS):
        out[g] = line


def last_kernel(parts, d_prompt, d_prompt_rope_t, d_resp, d_resp_rope_t):
    total = parts[0, :, EXT : 3 * EXT].astype(F32)
    for g in range(1, CHIPS):
        total = total + parts[g, :, EXT : 3 * EXT].astype(F32)
    page = jnp.concatenate([total[:, 0:EXT], total[:, EXT : 2 * EXT]], axis=0)
    d_prompt[...] = page[:, 0:DC]
    d_prompt_rope_t[...] = jnp.transpose(page[:, DC:EXT])[0:DR]
    rows = jnp.concatenate([parts[g, :, 0:EXT].astype(F32) for g in range(CHIPS)], axis=0)
    d_resp[...] = rows[:, 0:DC]
    d_resp_rope_t[...] = jnp.transpose(rows[:, DC:EXT])[0:DR]


def call(kernel, outs, *args, scratch=(), scalars=0):
    vmem = pl.BlockSpec(memory_space=pltpu.VMEM)
    smem = pl.BlockSpec(memory_space=pltpu.SMEM)
    return pl.pallas_call(
        kernel,
        out_shape=[jax.ShapeDtypeStruct(shape, kind) for shape, kind in outs],
        in_specs=[smem] * scalars + [vmem] * (len(args) - scalars),
        out_specs=[vmem] * len(outs),
        scratch_shapes=list(scratch),
        compiler_params=PARAMS,
    )(*args)


def spread(parts, axes):
    return lax.all_to_all(parts, axes, 0, 0, tiled=True)


def body(
    q_nope,
    q_rope,
    resp_latent,
    resp_rope_t,
    prompt_latent,
    prompt_rope_t,
    w_key_up,
    w_value_up,
    grad_out,
    lengths,
):
    swap = [(0, 1), (1, 0)]
    (pages,) = call(pages_kernel, [((CHIPS, PAGE, EXT), BF16)], prompt_latent, prompt_rope_t)
    own = spread(pages, ("xl", "y"))
    other = lax.ppermute(own, "c", swap)
    where = jnp.stack([lengths[0], lax.axis_index("c").astype(jnp.int32)])
    d_q_nope, d_q_rope, send_resp, keep, send = call(
        main_kernel,
        [
            ((RESP, LOCAL * DN), BF16),
            ((RESP, LOCAL * DR), BF16),
            ((CHIPS, 8, EXT), BF16),
            ((CHIPS, PAGE, WIDE), BF16),
            ((CHIPS, PAGE, WIDE), BF16),
        ],
        where,
        q_nope,
        q_rope,
        grad_out,
        w_key_up,
        w_value_up,
        own,
        other,
        resp_latent,
        resp_rope_t,
        scalars=1,
        scratch=[
            pltpu.VMEM((KEYS, EXT), BF16),
            pltpu.VMEM((ROWS, EXT), BF16),
            pltpu.VMEM((ROWS, DC), BF16),
            pltpu.VMEM((DC, 2 * LOCAL * DN), BF16),
            pltpu.VMEM((KEYS, EXT), BF16),
        ],
    )
    chip_sum = keep + lax.ppermute(send, "c", swap)
    head_parts = spread(send_resp, HEAD)
    sample_parts = spread(chip_sum, ("xl", "y"))
    d_key_up, d_value_up, line = call(
        middle_kernel,
        [
            ((PAGE, LOCAL * DN), F32),
            ((PAGE, LOCAL * DV), F32),
            ((CHIPS, 8, 3 * EXT), BF16),
        ],
        sample_parts,
        head_parts,
    )
    lines = spread(line, HEAD)
    d_prompt, d_prompt_rope_t, d_resp, d_resp_rope_t = call(
        last_kernel,
        [
            ((PAGE, DC), F32),
            ((DR, PAGE), F32),
            ((RESP, DC), F32),
            ((DR, RESP), F32),
        ],
        lines,
    )
    return (
        d_q_nope,
        d_q_rope,
        d_key_up,
        d_value_up,
        d_prompt,
        d_prompt_rope_t,
        d_resp,
        d_resp_rope_t,
    )


def solution(mesh):
    fine = Mesh(mesh.devices.reshape(2, 8, 2, 8, 2), SAMPLE + HEAD)
    return jax.shard_map(
        body,
        mesh=fine,
        in_specs=(
            P(SAMPLE, HEAD),
            P(SAMPLE, HEAD),
            P(SAMPLE, None),
            P(None, SAMPLE),
            P(SAMPLE, None),
            P(None, SAMPLE),
            P(None, HEAD),
            P(None, HEAD),
            P(SAMPLE, HEAD),
            P(SAMPLE),
        ),
        out_specs=(
            P(SAMPLE, HEAD),
            P(SAMPLE, HEAD),
            P(SAMPLE, HEAD),
            P(SAMPLE, HEAD),
            P(SAMPLE, None),
            P(None, SAMPLE),
            P(SAMPLE, None),
            P(None, SAMPLE),
        ),
        check_vma=False,
    )
```

```python
import functools

import jax
import jax.numpy as jnp
from jax import lax
from jax.experimental import pallas as pl
from jax.experimental.pallas import tpu as pltpu
from jax.sharding import Mesh, PartitionSpec as P

DC = 512
DR = 64
DN = 128
DV = 128
RESP = 128
PAGE = 16
LOCAL = 4
ROWS = LOCAL * RESP
EXT = 640
CHIPS = 16
HALF = CHIPS * PAGE
KEYS = 2 * HALF + RESP
WIDE = 2 * LOCAL * DN + EXT
OWNERS = [4 * (b & 1) + 2 * (b >> 1 & 1) + (b >> 2 & 1) for b in range(RESP // PAGE)]
SCALE = (DN + DR) ** (-0.5)
F32 = jnp.float32
BF16 = jnp.bfloat16
SAMPLE = ("xl", "y", "c")
HEAD = ("z", "xh")
PARAMS = pltpu.CompilerParams(vmem_limit_bytes=40 * 1024 * 1024)


def dot(a, b, ca, cb):
    return lax.dot_general(a, b, (((ca,), (cb,)), ((), ())), preferred_element_type=F32)


def columns(part, width):
    return slice(part * width, (part + 1) * width)


def with_rope(latent, rope):
    pad = jnp.zeros((latent.shape[0], EXT - DC - DR), BF16)
    return jnp.concatenate([latent, rope, pad], axis=1)


def pages_kernel(latent_far, rope_far, out, latent, rope, done):
    first = pltpu.make_async_copy(latent_far, latent, done.at[0])
    second = pltpu.make_async_copy(rope_far, rope, done.at[1])
    first.start()
    second.start()
    first.wait()
    second.wait()
    page = with_rope(latent[...], rope[...])
    for k in range(CHIPS):
        out[k] = page


def query_kernel(
    where,
    q_nope,
    q_rope,
    grad,
    w_key,
    w_value,
    resp_latent,
    resp_rope_t,
    query,
    d_out,
    masked_out,
    resp_keys,
):
    length = where[0]
    rope = jnp.transpose(resp_rope_t[...].astype(F32)).astype(BF16)
    resp_keys[...] = with_rope(resp_latent[...], rope)
    live = lax.broadcasted_iota(jnp.int32, (RESP, LOCAL * DV), 0) < length
    masked = jnp.where(live, grad[...].astype(F32), 0.0).astype(BF16)
    masked_out[...] = masked
    for h in range(LOCAL):
        rows = columns(h, RESP)
        latent = dot(q_nope[:, columns(h, DN)], w_key[:, columns(h, DN)], 1, 1)
        query[rows, :] = with_rope(latent.astype(BF16), q_rope[:, columns(h, DR)])
        d_out[rows, :] = dot(masked[:, columns(h, DV)], w_value[:, columns(h, DV)], 1, 1).astype(
            BF16
        )


def attention_kernel(
    where,
    query,
    d_out,
    own,
    other,
    resp_keys,
    keep_resp,
    send_resp,
    attention_out,
    d_scores_out,
    keys,
):
    length = where[0]
    keys[0:HALF, :] = own[...].reshape(HALF, EXT)
    keys[HALF : 2 * HALF, :] = other[...].reshape(HALF, EXT)
    keys[2 * HALF : KEYS, :] = resp_keys[...]
    scores = dot(keys[...], query[...], 1, 1) * SCALE
    token = lax.broadcasted_iota(jnp.int32, (RESP, ROWS), 1) % RESP
    key_at = lax.broadcasted_iota(jnp.int32, (RESP, ROWS), 0)
    allowed = (key_at <= token) & (key_at < length)
    scores = jnp.concatenate(
        [scores[0 : 2 * HALF], jnp.where(allowed, scores[2 * HALF : KEYS], -1e30)], axis=0
    )
    highest = jnp.max(scores, axis=0, keepdims=True)
    exponent = jnp.exp(scores - highest)
    attention = exponent * (1.0 / jnp.sum(exponent, axis=0, keepdims=True))
    attention_b = attention.astype(BF16)
    attention_out[...] = attention_b
    d_attention = dot(keys[:, 0:DC], d_out[...], 1, 1)
    row_delta = jnp.sum(attention * d_attention, axis=0, keepdims=True)
    d_scores = (SCALE * attention * (d_attention - row_delta)).astype(BF16)
    d_scores_out[...] = d_scores
    own_grad = dot(d_scores[2 * HALF : KEYS], query[...], 1, 0)
    own_grad_v = dot(attention_b[2 * HALF : KEYS], d_out[...], 1, 0)
    resp = jnp.concatenate([own_grad[:, 0:DC] + own_grad_v, own_grad[:, DC:EXT]], axis=1)
    blocks = resp.astype(BF16).reshape(RESP // PAGE, PAGE, EXT)
    place = where[2]
    for g in range(RESP // PAGE // 2):
        low, high = blocks[g], blocks[RESP // PAGE // 2 + g]
        keep_resp[g] = jnp.where(place == 0, low, high)
        send_resp[g] = jnp.where(place == 0, high, low)


def grads_kernel(
    where,
    q_nope,
    masked,
    query,
    d_out,
    keys,
    attention,
    d_scores,
    d_query_out,
    keep,
    send,
    weight,
    prompt,
):
    core = where[1]
    prompt_scores = d_scores[0 : 2 * HALF, :]
    key_grad = dot(prompt_scores, query[...], 1, 0)
    key_grad_v = dot(attention[0 : 2 * HALF, :], d_out[...], 1, 0)
    prompt[:, 0:DC] = (key_grad[:, 0:DC] + key_grad_v).astype(BF16)
    prompt[:, DC:EXT] = key_grad[:, DC:EXT].astype(BF16)
    d_query = dot(keys[...], d_scores[...], 0, 0).astype(BF16)
    d_query_out[...] = d_query
    out_latent = dot(keys[:, 0:DC], attention[...], 0, 0).astype(BF16)
    for h in range(LOCAL):
        d_q = d_query[0:DC, columns(h, RESP)]
        weight[:, columns(h, DN)] = dot(d_q, q_nope[:, columns(h, DN)], 1, 0).astype(BF16)
        weight[:, columns(LOCAL + h, DN)] = dot(
            out_latent[:, columns(h, RESP)], masked[:, columns(h, DV)], 1, 0
        ).astype(BF16)
    width = 2 * LOCAL * DN
    for k in range(CHIPS):
        mine = pl.ds(pl.multiple_of((2 * k + core) * PAGE, PAGE), PAGE)
        theirs = pl.ds(pl.multiple_of((2 * k + 1 - core) * PAGE, PAGE), PAGE)
        keep[k, :, 0:width] = weight[mine, :]
        send[k, :, 0:width] = weight[theirs, :]
        keep[k, :, width:WIDE] = prompt[k * PAGE : (k + 1) * PAGE, :]
        send[k, :, width:WIDE] = prompt[HALF + k * PAGE : HALF + (k + 1) * PAGE, :]


def query_grad_kernel(d_query, w_key, d_q_nope, d_q_rope):
    for h in range(LOCAL):
        d_q = d_query[0:DC, columns(h, RESP)]
        d_q_nope[:, columns(h, DN)] = dot(d_q, w_key[:, columns(h, DN)], 0, 0).astype(BF16)
    d_rope = jnp.concatenate(
        [
            jnp.transpose(d_query[DC : DC + DR, columns(h, RESP)].astype(F32)) for h in range(LOCAL)
        ],
        axis=1,
    )
    d_q_rope[...] = d_rope.astype(BF16)


def halve_kernel(bit, where, kept, received, keep, send):
    half = keep.shape[0]
    place = where[bit]
    mine = pl.ds(place * half, half)
    theirs = pl.ds((1 - place) * half, half)
    keep[...] = (kept[mine].astype(F32) + received[mine].astype(F32)).astype(BF16)
    send[...] = (kept[theirs].astype(F32) + received[theirs].astype(F32)).astype(BF16)


def middle_kernel(sample_parts, kept, received, d_key_up, d_value_up, out):
    total = sample_parts[0].astype(F32)
    for k in range(1, CHIPS):
        total = total + sample_parts[k].astype(F32)
    d_key_up[...] = total[:, 0 : LOCAL * DN]
    d_value_up[...] = total[:, LOCAL * DN : 2 * LOCAL * DN]
    page = total[:, 2 * LOCAL * DN : WIDE]
    rows = kept[0].astype(F32) + received[0].astype(F32)
    line = jnp.concatenate([rows, page], axis=1).astype(BF16)
    for g in range(CHIPS):
        out[g] = line


def last_kernel(parts, d_prompt, d_prompt_rope, d_resp, d_resp_rope_t):
    page = parts[0, :, EXT : 2 * EXT].astype(F32)
    for g in range(1, CHIPS):
        page = page + parts[g, :, EXT : 2 * EXT].astype(F32)
    d_prompt[...] = page[:, 0:DC]
    d_prompt_rope[...] = page[:, DC : DC + DR]
    rows = jnp.concatenate(
        [parts[g, :, 0:EXT].astype(F32) + parts[g + 8, :, 0:EXT].astype(F32) for g in OWNERS],
        axis=0,
    )
    d_resp[...] = rows[:, 0:DC]
    d_resp_rope_t[...] = jnp.transpose(rows[:, DC:EXT])[0:DR]


def call(kernel, outs, *args, scratch=(), scalars=0, flops=0, far=False):
    vmem = pl.BlockSpec(memory_space=pltpu.VMEM)
    smem = pl.BlockSpec(memory_space=pltpu.SMEM)
    return pl.pallas_call(
        kernel,
        out_shape=[jax.ShapeDtypeStruct(shape, kind) for shape, kind in outs],
        in_specs=[smem] * scalars + [pl.BlockSpec(memory_space=pl.ANY) if far else vmem] * (len(args) - scalars),
        out_specs=[vmem] * len(outs),
        scratch_shapes=list(scratch),
        compiler_params=PARAMS,
        cost_estimate=pl.CostEstimate(flops=flops, bytes_accessed=0, transcendentals=0),
    )(*args)


def spread(parts, axes):
    return lax.all_to_all(parts, axes, 0, 0, tiled=True)


def body(
    q_nope,
    q_rope,
    resp_latent,
    resp_rope_t,
    prompt_latent,
    prompt_rope_t,
    w_key_up,
    w_value_up,
    grad_out,
    lengths,
):
    swap = [(0, 1), (1, 0)]
    (pages,) = call(
        pages_kernel,
        [((CHIPS, PAGE, EXT), BF16)],
        prompt_latent,
        jnp.transpose(prompt_rope_t),
        far=True,
        scratch=[
            pltpu.VMEM((PAGE, DC), BF16),
            pltpu.VMEM((PAGE, DR), BF16),
            pltpu.SemaphoreType.DMA((2,)),
        ],
    )
    own = spread(pages, ("xl", "y"))
    z = lax.axis_index("z")
    where = jnp.stack(
        [lengths[0], lax.axis_index("c"), lax.axis_index("xh"), z & 1, z >> 1 & 1]
    )
    query, d_out, masked, resp_keys = call(
        query_kernel,
        [
            ((ROWS, EXT), BF16),
            ((ROWS, DC), BF16),
            ((RESP, LOCAL * DV), BF16),
            ((RESP, EXT), BF16),
        ],
        where,
        q_nope,
        q_rope,
        grad_out,
        w_key_up,
        w_value_up,
        resp_latent,
        resp_rope_t,
        scalars=1,
        flops=4_000_000_000,
    )
    own, query = lax.optimization_barrier((own, query))
    other = lax.ppermute(own, "c", swap)
    keep_resp, send_resp, attention, d_scores, keys = call(
        attention_kernel,
        [
            ((RESP // PAGE // 2, PAGE, EXT), BF16),
            ((RESP // PAGE // 2, PAGE, EXT), BF16),
            ((KEYS, ROWS), BF16),
            ((KEYS, ROWS), BF16),
            ((KEYS, EXT), BF16),
        ],
        where,
        query,
        d_out,
        own,
        other,
        resp_keys,
        scalars=1,
        flops=4_000_000_000,
    )
    got_resp = lax.ppermute(send_resp, "xh", swap)
    d_query, keep, send = call(
        grads_kernel,
        [
            ((EXT, ROWS), BF16),
            ((CHIPS, PAGE, WIDE), BF16),
            ((CHIPS, PAGE, WIDE), BF16),
        ],
        where,
        q_nope,
        masked,
        query,
        d_out,
        keys,
        attention,
        d_scores,
        scalars=1,
        flops=4_000_000_000,
        scratch=[
            pltpu.VMEM((DC, 2 * LOCAL * DN), BF16),
            pltpu.VMEM((2 * HALF, EXT), BF16),
        ],
    )
    chip_sum = keep + lax.ppermute(send, "c", swap)
    sample_parts = spread(chip_sum, ("xl", "y"))
    d_q_nope, d_q_rope = call(
        query_grad_kernel,
        [((RESP, LOCAL * DN), BF16), ((RESP, LOCAL * DR), BF16)],
        d_query,
        w_key_up,
        flops=1_000_000_000,
    )
    for bit in range(2):
        half = keep_resp.shape[0] // 2
        keep_resp, send_resp = call(
            functools.partial(halve_kernel, 3 + bit),
            [((half, PAGE, EXT), BF16)] * 2,
            where,
            keep_resp,
            got_resp,
            scalars=1,
        )
        got_resp = lax.ppermute(send_resp, "z", [(i, i ^ (1 << bit)) for i in range(8)])
    d_key_up, d_value_up, line = call(
        middle_kernel,
        [
            ((PAGE, LOCAL * DN), F32),
            ((PAGE, LOCAL * DV), F32),
            ((CHIPS, PAGE, 2 * EXT), BF16),
        ],
        sample_parts,
        keep_resp,
        got_resp,
    )
    lines = spread(line, HEAD)
    d_prompt, d_prompt_rope, d_resp, d_resp_rope_t = call(
        last_kernel,
        [
            ((PAGE, DC), F32),
            ((PAGE, DR), F32),
            ((RESP, DC), F32),
            ((DR, RESP), F32),
        ],
        lines,
    )
    return (
        d_q_nope,
        d_q_rope,
        d_key_up,
        d_value_up,
        d_prompt,
        jnp.transpose(d_prompt_rope),
        d_resp,
        d_resp_rope_t,
    )


def solution(mesh):
    fine = Mesh(mesh.devices.reshape(2, 8, 2, 8, 2), SAMPLE + HEAD)
    return jax.shard_map(
        body,
        mesh=fine,
        in_specs=(
            P(SAMPLE, HEAD),
            P(SAMPLE, HEAD),
            P(SAMPLE, None),
            P(None, SAMPLE),
            P(SAMPLE, None),
            P(None, SAMPLE),
            P(None, HEAD),
            P(None, HEAD),
            P(SAMPLE, HEAD),
            P(SAMPLE),
        ),
        out_specs=(
            P(SAMPLE, HEAD),
            P(SAMPLE, HEAD),
            P(SAMPLE, HEAD),
            P(SAMPLE, HEAD),
            P(SAMPLE, None),
            P(None, SAMPLE),
            P(SAMPLE, None),
            P(None, SAMPLE),
        ),
        check_vma=False,
    )
```

```python
import functools

import jax
import jax.numpy as jnp
from jax import lax
from jax.experimental import pallas as pl
from jax.experimental.pallas import tpu as pltpu
from jax.sharding import Mesh, PartitionSpec as P

DC = 512
DR = 64
DN = 128
DV = 128
RESP = 128
PAGE = 16
LOCAL = 4
ROWS = LOCAL * RESP
EXT = 640
KEY = DC + DR
CHIPS = 16
HALF = CHIPS * PAGE
KEYS = 2 * HALF + RESP
WIDE = 2 * LOCAL * DN + EXT
OWNERS = [1 * (b & 1) + 4 * (b >> 1 & 1) + 2 * (b >> 2 & 1) for b in range(RESP // PAGE)]
SCALE = (DN + DR) ** (-0.5)
F32 = jnp.float32
BF16 = jnp.bfloat16
SAMPLE = ("xl", "y", "c")
HEAD = ("z", "xh")
PARAMS = pltpu.CompilerParams(vmem_limit_bytes=40 * 1024 * 1024)


def dot(a, b, ca, cb):
    return lax.dot_general(a, b, (((ca,), (cb,)), ((), ())), preferred_element_type=F32)


def columns(part, width):
    return slice(part * width, (part + 1) * width)


def with_rope(latent, rope):
    pad = jnp.zeros((latent.shape[0], EXT - DC - DR), BF16)
    return jnp.concatenate([latent, rope, pad], axis=1)


def pages_kernel(latent_far, rope_far, out, latent, rope, done):
    first = pltpu.make_async_copy(latent_far, latent, done.at[0])
    second = pltpu.make_async_copy(rope_far, rope, done.at[1])
    first.start()
    second.start()
    first.wait()
    second.wait()
    page = with_rope(latent[...], rope[...])
    for k in range(CHIPS):
        out[k] = page


def query_kernel(
    where,
    q_nope,
    q_rope,
    grad,
    w_key,
    w_value,
    resp_latent,
    resp_rope_t,
    query,
    d_out,
    masked_out,
    resp_keys,
):
    length = where[0]
    rope = jnp.transpose(resp_rope_t[...].astype(F32)).astype(BF16)
    resp_keys[...] = with_rope(resp_latent[...], rope)
    live = lax.broadcasted_iota(jnp.int32, (RESP, LOCAL * DV), 0) < length
    masked = jnp.where(live, grad[...].astype(F32), 0.0).astype(BF16)
    masked_out[...] = masked
    for h in range(LOCAL):
        rows = columns(h, RESP)
        latent = dot(q_nope[:, columns(h, DN)], w_key[:, columns(h, DN)], 1, 1)
        query[rows, :] = with_rope(latent.astype(BF16), q_rope[:, columns(h, DR)])
        d_out[rows, :] = dot(masked[:, columns(h, DV)], w_value[:, columns(h, DV)], 1, 1).astype(
            BF16
        )


def first_scores_kernel(where, query, d_out, own, resp_keys, scores, d_attention):
    length = where[0]
    pages = own[...].reshape(HALF, EXT)
    resp = resp_keys[...]
    scores[0:HALF, :] = dot(pages, query[...], 1, 1) * SCALE
    token = lax.broadcasted_iota(jnp.int32, (RESP, ROWS), 1) % RESP
    key_at = lax.broadcasted_iota(jnp.int32, (RESP, ROWS), 0)
    allowed = (key_at <= token) & (key_at < length)
    own_scores = dot(resp, query[...], 1, 1) * SCALE
    scores[HALF : HALF + RESP, :] = jnp.where(allowed, own_scores, -1e30)
    d_attention[0:HALF, :] = dot(pages[:, 0:DC], d_out[...], 1, 1)
    d_attention[HALF : HALF + RESP, :] = dot(resp[:, 0:DC], d_out[...], 1, 1)


def attention_kernel(
    where,
    query,
    d_out,
    own,
    other,
    resp_keys,
    first_scores,
    first_d_attention,
    keep_resp,
    send_resp,
    attention_out,
    d_scores_out,
    keys,
):
    keys[0:HALF, :] = own[...].reshape(HALF, EXT)
    keys[HALF : 2 * HALF, :] = other[...].reshape(HALF, EXT)
    keys[2 * HALF : KEYS, :] = resp_keys[...]
    other_rows = other[...].reshape(HALF, EXT)
    other_scores = dot(other_rows, query[...], 1, 1) * SCALE
    scores = jnp.concatenate(
        [first_scores[0:HALF], other_scores, first_scores[HALF : HALF + RESP]], axis=0
    )
    highest = jnp.max(scores, axis=0, keepdims=True)
    exponent = jnp.exp(scores - highest)
    attention = exponent * (1.0 / jnp.sum(exponent, axis=0, keepdims=True))
    attention_b = attention.astype(BF16)
    attention_out[...] = attention_b
    d_attention = jnp.concatenate(
        [
            first_d_attention[0:HALF],
            dot(other_rows[:, 0:DC], d_out[...], 1, 1),
            first_d_attention[HALF : HALF + RESP],
        ],
        axis=0,
    )
    row_delta = jnp.sum(attention * d_attention, axis=0, keepdims=True)
    d_scores = (SCALE * attention * (d_attention - row_delta)).astype(BF16)
    d_scores_out[...] = d_scores
    own_grad = dot(d_scores[2 * HALF : KEYS], query[...], 1, 0)
    own_grad_v = dot(attention_b[2 * HALF : KEYS], d_out[...], 1, 0)
    resp = jnp.concatenate([own_grad[:, 0:DC] + own_grad_v, own_grad[:, DC:EXT]], axis=1)
    blocks = resp.astype(BF16).reshape(RESP // PAGE, PAGE, EXT)
    place = where[2]
    for g in range(RESP // PAGE // 2):
        low, high = blocks[g], blocks[RESP // PAGE // 2 + g]
        keep_resp[g] = jnp.where(place == 0, low, high)
        send_resp[g] = jnp.where(place == 0, high, low)


def half_grads(parity, first_key, q_nope, masked, query, d_out, attention, d_scores, d_query, out_latent, out):
    starts = [pl.multiple_of((2 * k + parity) * PAGE, PAGE) for k in range(CHIPS)]
    d_q = jnp.concatenate([d_query[pl.ds(start, PAGE), :] for start in starts], axis=0)
    values = jnp.concatenate([out_latent[pl.ds(start, PAGE), :] for start in starts], axis=0)
    for h in range(LOCAL):
        key_part = dot(d_q[:, columns(h, RESP)], q_nope[:, columns(h, DN)], 1, 0)
        out[:, :, columns(h, DN)] = key_part.astype(BF16).reshape(CHIPS, PAGE, DN)
        value_part = dot(values[:, columns(h, RESP)], masked[:, columns(h, DV)], 1, 0)
        out[:, :, columns(LOCAL + h, DN)] = value_part.astype(BF16).reshape(CHIPS, PAGE, DN)
    rows = slice(first_key, first_key + HALF)
    key_grad = dot(d_scores[rows, :], query[...], 1, 0)
    key_grad_v = dot(attention[rows, :], d_out[...], 1, 0)
    width = 2 * LOCAL * DN
    latent_part = (key_grad[:, 0:DC] + key_grad_v).astype(BF16)
    out[:, :, width : width + DC] = latent_part.reshape(CHIPS, PAGE, DC)
    out[:, :, width + DC : WIDE] = key_grad[:, DC:EXT].astype(BF16).reshape(CHIPS, PAGE, EXT - DC)


def send_kernel(
    where,
    q_nope,
    masked,
    query,
    d_out,
    keys,
    attention,
    d_scores,
    d_query,
    out_latent,
    send,
):
    d_query[...] = dot(keys[...], d_scores[...], 0, 0).astype(BF16)
    out_latent[...] = dot(keys[:, 0:DC], attention[...], 0, 0).astype(BF16)
    half_grads(1 - where[1], HALF, q_nope, masked, query, d_out, attention, d_scores, d_query, out_latent, send)


def keep_kernel(
    where, q_nope, masked, query, d_out, attention, d_scores, d_query, out_latent, keep
):
    half_grads(where[1], 0, q_nope, masked, query, d_out, attention, d_scores, d_query, out_latent, keep)


def query_grad_kernel(d_query, w_key, d_q_nope, d_q_rope):
    for h in range(LOCAL):
        d_q = d_query[0:DC, columns(h, RESP)]
        d_q_nope[:, columns(h, DN)] = dot(d_q, w_key[:, columns(h, DN)], 0, 0).astype(BF16)
    d_rope = jnp.concatenate(
        [
            jnp.transpose(d_query[DC : DC + DR, columns(h, RESP)].astype(F32)) for h in range(LOCAL)
        ],
        axis=1,
    )
    d_q_rope[...] = d_rope.astype(BF16)


def halve_kernel(bit, where, kept, received, keep, send):
    half = keep.shape[0]
    place = where[bit]
    mine = pl.ds(place * half, half)
    theirs = pl.ds((1 - place) * half, half)
    keep[...] = (kept[mine].astype(F32) + received[mine].astype(F32)).astype(BF16)
    send[...] = (kept[theirs].astype(F32) + received[theirs].astype(F32)).astype(BF16)


def line_kernel(sample_parts, kept, received, out):
    first = 2 * LOCAL * DN
    page = sample_parts[0, :, first:WIDE].astype(F32)
    for k in range(1, CHIPS):
        page = page + sample_parts[k, :, first:WIDE].astype(F32)
    rows = kept[0].astype(F32) + received[0].astype(F32)
    line = jnp.concatenate([rows[:, 0:KEY], page[:, 0:KEY]], axis=1).astype(BF16)
    for g in range(CHIPS):
        out[g] = line


def weights_kernel(sample_parts, d_key_up, d_value_up):
    for out, first in ((d_key_up, 0), (d_value_up, LOCAL * DN)):
        lanes = slice(first, first + LOCAL * DN)
        total = sample_parts[0, :, lanes].astype(F32)
        for k in range(1, CHIPS):
            total = total + sample_parts[k, :, lanes].astype(F32)
        out[...] = total


def last_kernel(parts, d_prompt, d_prompt_rope, d_resp, d_resp_rope_t):
    page = parts[0].astype(F32)
    for g in range(1, CHIPS):
        page = page + parts[g].astype(F32)
    d_prompt[...] = page[:, KEY : KEY + DC]
    d_prompt_rope[...] = page[:, KEY + DC : 2 * KEY]
    rows = jnp.concatenate(
        [parts[g, :, 0:KEY].astype(F32) + parts[g + 8, :, 0:KEY].astype(F32) for g in OWNERS],
        axis=0,
    )
    d_resp[...] = rows[:, 0:DC]
    d_resp_rope_t[...] = jnp.transpose(rows[:, DC:KEY])


def call(kernel, outs, *args, scratch=(), scalars=0, flops=0, far=False):
    vmem = pl.BlockSpec(memory_space=pltpu.VMEM)
    smem = pl.BlockSpec(memory_space=pltpu.SMEM)
    return pl.pallas_call(
        kernel,
        out_shape=[jax.ShapeDtypeStruct(shape, kind) for shape, kind in outs],
        in_specs=[smem] * scalars + [pl.BlockSpec(memory_space=pltpu.HBM) if far else vmem] * (len(args) - scalars),
        out_specs=[vmem] * len(outs),
        scratch_shapes=list(scratch),
        compiler_params=PARAMS,
        cost_estimate=pl.CostEstimate(flops=flops, bytes_accessed=0, transcendentals=0),
    )(*args)


def spread(parts, axes):
    return lax.all_to_all(parts, axes, 0, 0, tiled=True)


def body(
    q_nope,
    q_rope,
    resp_latent,
    resp_rope_t,
    prompt_latent,
    prompt_rope_t,
    w_key_up,
    w_value_up,
    grad_out,
    lengths,
):
    swap = [(0, 1), (1, 0)]
    (pages,) = call(
        pages_kernel,
        [((CHIPS, PAGE, EXT), BF16)],
        pltpu.with_memory_space_constraint(prompt_latent, pltpu.HBM),
        pltpu.with_memory_space_constraint(jnp.transpose(prompt_rope_t), pltpu.HBM),
        far=True,
        scratch=[
            pltpu.VMEM((PAGE, DC), BF16),
            pltpu.VMEM((PAGE, DR), BF16),
            pltpu.SemaphoreType.DMA((2,)),
        ],
    )
    own = spread(pages, ("xl", "y"))
    z = lax.axis_index("z")
    where = jnp.stack(
        [lengths[0], lax.axis_index("c"), z & 1, z >> 1 & 1, lax.axis_index("xh")]
    )
    query, d_out, masked, resp_keys = call(
        query_kernel,
        [
            ((ROWS, EXT), BF16),
            ((ROWS, DC), BF16),
            ((RESP, LOCAL * DV), BF16),
            ((RESP, EXT), BF16),
        ],
        where,
        q_nope,
        q_rope,
        grad_out,
        w_key_up,
        w_value_up,
        resp_latent,
        resp_rope_t,
        scalars=1,
        flops=4_000_000_000,
    )
    own, query = lax.optimization_barrier((own, query))
    other = lax.ppermute(own, "c", swap)
    first_scores, first_d_attention = call(
        first_scores_kernel,
        [((HALF + RESP, ROWS), F32)] * 2,
        where,
        query,
        d_out,
        own,
        resp_keys,
        scalars=1,
        flops=2_000_000_000,
    )
    keep_resp, send_resp, attention, d_scores, keys = call(
        attention_kernel,
        [
            ((RESP // PAGE // 2, PAGE, EXT), BF16),
            ((RESP // PAGE // 2, PAGE, EXT), BF16),
            ((KEYS, ROWS), BF16),
            ((KEYS, ROWS), BF16),
            ((KEYS, EXT), BF16),
        ],
        where,
        query,
        d_out,
        own,
        other,
        resp_keys,
        first_scores,
        first_d_attention,
        scalars=1,
        flops=4_000_000_000,
    )
    got_resp = lax.ppermute(send_resp, "z", [(i, i ^ 1) for i in range(8)])
    d_query, out_latent, send = call(
        send_kernel,
        [
            ((EXT, ROWS), BF16),
            ((DC, ROWS), BF16),
            ((CHIPS, PAGE, WIDE), BF16),
        ],
        where,
        q_nope,
        masked,
        query,
        d_out,
        keys,
        attention,
        d_scores,
        scalars=1,
        flops=4_000_000_000,
    )
    (keep,) = call(
        keep_kernel,
        [((CHIPS, PAGE, WIDE), BF16)],
        where,
        q_nope,
        masked,
        query,
        d_out,
        attention,
        d_scores,
        d_query,
        out_latent,
        scalars=1,
        flops=2_000_000_000,
    )
    chip_sum = keep + lax.ppermute(send, "c", swap)
    sample_parts = spread(chip_sum, ("xl", "y"))
    d_q_nope, d_q_rope = call(
        query_grad_kernel,
        [((RESP, LOCAL * DN), BF16), ((RESP, LOCAL * DR), BF16)],
        d_query,
        w_key_up,
        flops=1_000_000_000,
    )
    keep_resp, send_resp = call(
        functools.partial(halve_kernel, 3),
        [((2, PAGE, EXT), BF16)] * 2,
        where,
        keep_resp,
        got_resp,
        scalars=1,
    )
    got_resp = lax.ppermute(send_resp, "z", [(i, i ^ 2) for i in range(8)])
    keep_resp, send_resp = call(
        functools.partial(halve_kernel, 4),
        [((1, PAGE, EXT), BF16)] * 2,
        where,
        keep_resp,
        got_resp,
        scalars=1,
    )
    got_resp = lax.ppermute(send_resp, "xh", swap)
    (line,) = call(
        line_kernel,
        [((CHIPS, PAGE, 2 * KEY), BF16)],
        sample_parts,
        keep_resp,
        got_resp,
    )
    d_key_up, d_value_up = call(
        weights_kernel,
        [((PAGE, LOCAL * DN), F32), ((PAGE, LOCAL * DV), F32)],
        sample_parts,
        flops=1_000_000_000,
    )
    lines = spread(line, HEAD)
    d_prompt, d_prompt_rope, d_resp, d_resp_rope_t = call(
        last_kernel,
        [
            ((PAGE, DC), F32),
            ((PAGE, DR), F32),
            ((RESP, DC), F32),
            ((DR, RESP), F32),
        ],
        lines,
    )
    return (
        d_q_nope,
        d_q_rope,
        d_key_up,
        d_value_up,
        d_prompt,
        jnp.transpose(d_prompt_rope),
        d_resp,
        d_resp_rope_t,
    )


def solution(mesh):
    fine = Mesh(mesh.devices.reshape(2, 8, 2, 8, 2), SAMPLE + HEAD)
    return jax.shard_map(
        body,
        mesh=fine,
        in_specs=(
            P(SAMPLE, HEAD),
            P(SAMPLE, HEAD),
            P(SAMPLE, None),
            P(None, SAMPLE),
            P(SAMPLE, None),
            P(None, SAMPLE),
            P(None, HEAD),
            P(None, HEAD),
            P(SAMPLE, HEAD),
            P(SAMPLE),
        ),
        out_specs=(
            P(SAMPLE, HEAD),
            P(SAMPLE, HEAD),
            P(SAMPLE, HEAD),
            P(SAMPLE, HEAD),
            P(SAMPLE, None),
            P(None, SAMPLE),
            P(SAMPLE, None),
            P(None, SAMPLE),
        ),
        check_vma=False,
    )
```

```python
import functools

import jax
import jax.numpy as jnp
from jax import lax
from jax.experimental import pallas as pl
from jax.experimental.pallas import tpu as pltpu
from jax.sharding import Mesh, PartitionSpec as P

DC = 512
DR = 64
DN = 128
DV = 128
RESP = 128
PAGE = 16
LOCAL = 4
ROWS = LOCAL * RESP
EXT = 640
KEY = DC + DR
CHIPS = 16
HALF = CHIPS * PAGE
KEYS = 2 * HALF + RESP
WIDE = 2 * LOCAL * DN + EXT
OWNERS = [8 * (b & 1) + 2 * (b >> 1 & 1) + (b >> 2 & 1) for b in range(RESP // PAGE)]
SCALE = (DN + DR) ** (-0.5)
F32 = jnp.float32
BF16 = jnp.bfloat16
SAMPLE = ("xl", "y", "c")
HEAD = ("z", "xh")
PARAMS = pltpu.CompilerParams(vmem_limit_bytes=40 * 1024 * 1024)


def dot(a, b, ca, cb):
    return lax.dot_general(a, b, (((ca,), (cb,)), ((), ())), preferred_element_type=F32)


def columns(part, width):
    return slice(part * width, (part + 1) * width)


def with_rope(latent, rope):
    pad = jnp.zeros((latent.shape[0], EXT - DC - DR), BF16)
    return jnp.concatenate([latent, rope, pad], axis=1)


def pages_kernel(latent_far, rope_far, out, latent, rope, done):
    first = pltpu.make_async_copy(latent_far, latent, done.at[0])
    second = pltpu.make_async_copy(rope_far, rope, done.at[1])
    first.start()
    second.start()
    first.wait()
    second.wait()
    page = with_rope(latent[...], rope[...])
    for k in range(CHIPS):
        out[k] = page


def query_kernel(
    where,
    q_nope,
    q_rope,
    grad,
    w_key,
    w_value,
    resp_latent,
    resp_rope_t,
    query,
    d_out,
    masked_out,
    resp_keys,
):
    length = where[0]
    rope = jnp.transpose(resp_rope_t[...].astype(F32)).astype(BF16)
    resp_keys[...] = with_rope(resp_latent[...], rope)
    live = lax.broadcasted_iota(jnp.int32, (RESP, LOCAL * DV), 0) < length
    masked = jnp.where(live, grad[...].astype(F32), 0.0).astype(BF16)
    masked_out[...] = masked
    for h in range(LOCAL):
        rows = columns(h, RESP)
        latent = dot(q_nope[:, columns(h, DN)], w_key[:, columns(h, DN)], 1, 1)
        query[rows, :] = with_rope(latent.astype(BF16), q_rope[:, columns(h, DR)])
        d_out[rows, :] = dot(masked[:, columns(h, DV)], w_value[:, columns(h, DV)], 1, 1).astype(
            BF16
        )


def first_scores_kernel(where, query, d_out, own, resp_keys, scores, d_attention):
    length = where[0]
    pages = own[...].reshape(HALF, EXT)
    resp = resp_keys[...]
    scores[0:HALF, :] = dot(pages, query[...], 1, 1) * SCALE
    token = lax.broadcasted_iota(jnp.int32, (RESP, ROWS), 1) % RESP
    key_at = lax.broadcasted_iota(jnp.int32, (RESP, ROWS), 0)
    allowed = (key_at <= token) & (key_at < length)
    own_scores = dot(resp, query[...], 1, 1) * SCALE
    scores[HALF : HALF + RESP, :] = jnp.where(allowed, own_scores, -1e30)
    d_attention[0:HALF, :] = dot(pages[:, 0:DC], d_out[...], 1, 1)
    d_attention[HALF : HALF + RESP, :] = dot(resp[:, 0:DC], d_out[...], 1, 1)


def attention_kernel(
    where,
    query,
    d_out,
    own,
    other,
    resp_keys,
    first_scores,
    first_d_attention,
    keep_resp,
    send_resp,
    attention_out,
    d_scores_out,
    keys,
):
    keys[0:HALF, :] = own[...].reshape(HALF, EXT)
    keys[HALF : 2 * HALF, :] = other[...].reshape(HALF, EXT)
    keys[2 * HALF : KEYS, :] = resp_keys[...]
    other_rows = other[...].reshape(HALF, EXT)
    other_scores = dot(other_rows, query[...], 1, 1) * SCALE
    scores = jnp.concatenate(
        [first_scores[0:HALF], other_scores, first_scores[HALF : HALF + RESP]], axis=0
    )
    highest = jnp.max(scores, axis=0, keepdims=True)
    exponent = jnp.exp(scores - highest)
    attention = exponent * (1.0 / jnp.sum(exponent, axis=0, keepdims=True))
    attention_b = attention.astype(BF16)
    attention_out[...] = attention_b
    d_attention = jnp.concatenate(
        [
            first_d_attention[0:HALF],
            dot(other_rows[:, 0:DC], d_out[...], 1, 1),
            first_d_attention[HALF : HALF + RESP],
        ],
        axis=0,
    )
    row_delta = jnp.sum(attention * d_attention, axis=0, keepdims=True)
    d_scores = (SCALE * attention * (d_attention - row_delta)).astype(BF16)
    d_scores_out[...] = d_scores
    own_grad = dot(d_scores[2 * HALF : KEYS], query[...], 1, 0)
    own_grad_v = dot(attention_b[2 * HALF : KEYS], d_out[...], 1, 0)
    resp = jnp.concatenate([own_grad[:, 0:DC] + own_grad_v, own_grad[:, DC:EXT]], axis=1)
    blocks = resp.astype(BF16).reshape(RESP // PAGE, PAGE, EXT)
    place = where[2]
    for g in range(RESP // PAGE // 2):
        low, high = blocks[g], blocks[RESP // PAGE // 2 + g]
        keep_resp[g] = jnp.where(place == 0, low, high)
        send_resp[g] = jnp.where(place == 0, high, low)


def half_grads(parity, first_key, q_nope, masked, query, d_out, attention, d_scores, d_query, out_latent, out):
    starts = [pl.multiple_of((2 * k + parity) * PAGE, PAGE) for k in range(CHIPS)]
    d_q = jnp.concatenate([d_query[pl.ds(start, PAGE), :] for start in starts], axis=0)
    values = jnp.concatenate([out_latent[pl.ds(start, PAGE), :] for start in starts], axis=0)
    for h in range(LOCAL):
        key_part = dot(d_q[:, columns(h, RESP)], q_nope[:, columns(h, DN)], 1, 0)
        out[:, :, columns(h, DN)] = key_part.astype(BF16).reshape(CHIPS, PAGE, DN)
        value_part = dot(values[:, columns(h, RESP)], masked[:, columns(h, DV)], 1, 0)
        out[:, :, columns(LOCAL + h, DN)] = value_part.astype(BF16).reshape(CHIPS, PAGE, DN)
    rows = slice(first_key, first_key + HALF)
    key_grad = dot(d_scores[rows, :], query[...], 1, 0)
    key_grad_v = dot(attention[rows, :], d_out[...], 1, 0)
    width = 2 * LOCAL * DN
    latent_part = (key_grad[:, 0:DC] + key_grad_v).astype(BF16)
    out[:, :, width : width + DC] = latent_part.reshape(CHIPS, PAGE, DC)
    out[:, :, width + DC : WIDE] = key_grad[:, DC:EXT].astype(BF16).reshape(CHIPS, PAGE, EXT - DC)


def send_kernel(
    where,
    q_nope,
    masked,
    query,
    d_out,
    keys,
    attention,
    d_scores,
    d_query,
    out_latent,
    send,
):
    d_query[...] = dot(keys[...], d_scores[...], 0, 0).astype(BF16)
    out_latent[...] = dot(keys[:, 0:DC], attention[...], 0, 0).astype(BF16)
    half_grads(1 - where[1], HALF, q_nope, masked, query, d_out, attention, d_scores, d_query, out_latent, send)


def keep_kernel(
    where, q_nope, masked, query, d_out, attention, d_scores, d_query, out_latent, keep
):
    half_grads(where[1], 0, q_nope, masked, query, d_out, attention, d_scores, d_query, out_latent, keep)


def query_grad_kernel(d_query, w_key, d_q_nope, d_q_rope):
    for h in range(LOCAL):
        d_q = d_query[0:DC, columns(h, RESP)]
        d_q_nope[:, columns(h, DN)] = dot(d_q, w_key[:, columns(h, DN)], 0, 0).astype(BF16)
    d_rope = jnp.concatenate(
        [
            jnp.transpose(d_query[DC : DC + DR, columns(h, RESP)].astype(F32)) for h in range(LOCAL)
        ],
        axis=1,
    )
    d_q_rope[...] = d_rope.astype(BF16)


def halve_kernel(bit, where, kept, received, keep, send):
    half = keep.shape[0]
    place = where[bit]
    mine = pl.ds(place * half, half)
    theirs = pl.ds((1 - place) * half, half)
    keep[...] = (kept[mine].astype(F32) + received[mine].astype(F32)).astype(BF16)
    send[...] = (kept[theirs].astype(F32) + received[theirs].astype(F32)).astype(BF16)


def line_kernel(sample_parts, kept, received, out):
    first = 2 * LOCAL * DN
    page = sample_parts[0, :, first:WIDE].astype(F32)
    for k in range(1, CHIPS):
        page = page + sample_parts[k, :, first:WIDE].astype(F32)
    rows = kept[0].astype(F32) + received[0].astype(F32)
    line = jnp.concatenate([rows[:, 0:KEY], page[:, 0:KEY]], axis=1).astype(BF16)
    for g in range(CHIPS):
        out[g] = line


def weights_kernel(sample_parts, d_key_up, d_value_up):
    for out, first in ((d_key_up, 0), (d_value_up, LOCAL * DN)):
        lanes = slice(first, first + LOCAL * DN)
        total = sample_parts[0, :, lanes].astype(F32)
        for k in range(1, CHIPS):
            total = total + sample_parts[k, :, lanes].astype(F32)
        out[...] = total


def last_kernel(parts, d_prompt, d_prompt_rope, d_resp, d_resp_rope_t):
    page = parts[0].astype(F32)
    for g in range(1, CHIPS):
        page = page + parts[g].astype(F32)
    d_prompt[...] = page[:, KEY : KEY + DC]
    d_prompt_rope[...] = page[:, KEY + DC : 2 * KEY]
    rows = jnp.concatenate(
        [parts[g, :, 0:KEY].astype(F32) + parts[g + 4, :, 0:KEY].astype(F32) for g in OWNERS],
        axis=0,
    )
    d_resp[...] = rows[:, 0:DC]
    d_resp_rope_t[...] = jnp.transpose(rows[:, DC:KEY])


def call(kernel, outs, *args, scratch=(), scalars=0, flops=0, far=False):
    vmem = pl.BlockSpec(memory_space=pltpu.VMEM)
    smem = pl.BlockSpec(memory_space=pltpu.SMEM)
    return pl.pallas_call(
        kernel,
        out_shape=[jax.ShapeDtypeStruct(shape, kind) for shape, kind in outs],
        in_specs=[smem] * scalars + [pl.BlockSpec(memory_space=pltpu.HBM) if far else vmem] * (len(args) - scalars),
        out_specs=[vmem] * len(outs),
        scratch_shapes=list(scratch),
        compiler_params=PARAMS,
        cost_estimate=pl.CostEstimate(flops=flops, bytes_accessed=0, transcendentals=0),
    )(*args)


def spread(parts, axes):
    return lax.all_to_all(parts, axes, 0, 0, tiled=True)


def body(
    q_nope,
    q_rope,
    resp_latent,
    resp_rope_t,
    prompt_latent,
    prompt_rope_t,
    w_key_up,
    w_value_up,
    grad_out,
    lengths,
):
    swap = [(0, 1), (1, 0)]
    (pages,) = call(
        pages_kernel,
        [((CHIPS, PAGE, EXT), BF16)],
        pltpu.with_memory_space_constraint(prompt_latent, pltpu.HBM),
        pltpu.with_memory_space_constraint(jnp.transpose(prompt_rope_t), pltpu.HBM),
        far=True,
        scratch=[
            pltpu.VMEM((PAGE, DC), BF16),
            pltpu.VMEM((PAGE, DR), BF16),
            pltpu.SemaphoreType.DMA((2,)),
        ],
    )
    own = spread(pages, ("xl", "y"))
    z = lax.axis_index("z")
    where = jnp.stack(
        [lengths[0], lax.axis_index("c"), z & 1, z >> 1 & 1, lax.axis_index("xh")]
    )
    query, d_out, masked, resp_keys = call(
        query_kernel,
        [
            ((ROWS, EXT), BF16),
            ((ROWS, DC), BF16),
            ((RESP, LOCAL * DV), BF16),
            ((RESP, EXT), BF16),
        ],
        where,
        q_nope,
        q_rope,
        grad_out,
        w_key_up,
        w_value_up,
        resp_latent,
        resp_rope_t,
        scalars=1,
        flops=4_000_000_000,
    )
    own, query = lax.optimization_barrier((own, query))
    other = lax.ppermute(own, "c", swap)
    first_scores, first_d_attention = call(
        first_scores_kernel,
        [((HALF + RESP, ROWS), F32)] * 2,
        where,
        query,
        d_out,
        own,
        resp_keys,
        scalars=1,
        flops=2_000_000_000,
    )
    keep_resp, send_resp, attention, d_scores, keys = call(
        attention_kernel,
        [
            ((RESP // PAGE // 2, PAGE, EXT), BF16),
            ((RESP // PAGE // 2, PAGE, EXT), BF16),
            ((KEYS, ROWS), BF16),
            ((KEYS, ROWS), BF16),
            ((KEYS, EXT), BF16),
        ],
        where,
        query,
        d_out,
        own,
        other,
        resp_keys,
        first_scores,
        first_d_attention,
        scalars=1,
        flops=4_000_000_000,
    )
    got_resp = lax.ppermute(send_resp, "z", [(i, i ^ 1) for i in range(8)])
    d_query, out_latent, send = call(
        send_kernel,
        [
            ((EXT, ROWS), BF16),
            ((DC, ROWS), BF16),
            ((CHIPS, PAGE, WIDE), BF16),
        ],
        where,
        q_nope,
        masked,
        query,
        d_out,
        keys,
        attention,
        d_scores,
        scalars=1,
        flops=4_000_000_000,
    )
    (keep,) = call(
        keep_kernel,
        [((CHIPS, PAGE, WIDE), BF16)],
        where,
        q_nope,
        masked,
        query,
        d_out,
        attention,
        d_scores,
        d_query,
        out_latent,
        scalars=1,
        flops=2_000_000_000,
    )
    chip_sum = keep + lax.ppermute(send, "c", swap)
    sample_parts = spread(chip_sum, ("xl", "y"))
    d_q_nope, d_q_rope = call(
        query_grad_kernel,
        [((RESP, LOCAL * DN), BF16), ((RESP, LOCAL * DR), BF16)],
        d_query,
        w_key_up,
        flops=1_000_000_000,
    )
    keep_resp, send_resp = call(
        functools.partial(halve_kernel, 3),
        [((2, PAGE, EXT), BF16)] * 2,
        where,
        keep_resp,
        got_resp,
        scalars=1,
    )
    got_resp = lax.ppermute(send_resp, "z", [(i, i ^ 2) for i in range(8)])
    keep_resp, send_resp = call(
        functools.partial(halve_kernel, 4),
        [((1, PAGE, EXT), BF16)] * 2,
        where,
        keep_resp,
        got_resp,
        scalars=1,
    )
    got_resp = lax.ppermute(send_resp, "xh", swap)
    (line,) = call(
        line_kernel,
        [((CHIPS, PAGE, 2 * KEY), BF16)],
        sample_parts,
        keep_resp,
        got_resp,
    )
    d_key_up, d_value_up = call(
        weights_kernel,
        [((PAGE, LOCAL * DN), F32), ((PAGE, LOCAL * DV), F32)],
        sample_parts,
        flops=1_000_000_000,
    )
    lines = spread(line, ("xh", "z"))
    d_prompt, d_prompt_rope, d_resp, d_resp_rope_t = call(
        last_kernel,
        [
            ((PAGE, DC), F32),
            ((PAGE, DR), F32),
            ((RESP, DC), F32),
            ((DR, RESP), F32),
        ],
        lines,
    )
    return (
        d_q_nope,
        d_q_rope,
        d_key_up,
        d_value_up,
        d_prompt,
        jnp.transpose(d_prompt_rope),
        d_resp,
        d_resp_rope_t,
    )


def solution(mesh):
    fine = Mesh(mesh.devices.reshape(2, 8, 2, 8, 2), SAMPLE + HEAD)
    return jax.shard_map(
        body,
        mesh=fine,
        in_specs=(
            P(SAMPLE, HEAD),
            P(SAMPLE, HEAD),
            P(SAMPLE, None),
            P(None, SAMPLE),
            P(SAMPLE, None),
            P(None, SAMPLE),
            P(None, HEAD),
            P(None, HEAD),
            P(SAMPLE, HEAD),
            P(SAMPLE),
        ),
        out_specs=(
            P(SAMPLE, HEAD),
            P(SAMPLE, HEAD),
            P(SAMPLE, HEAD),
            P(SAMPLE, HEAD),
            P(SAMPLE, None),
            P(None, SAMPLE),
            P(SAMPLE, None),
            P(None, SAMPLE),
        ),
        check_vma=False,
    )
```

```python
import functools

import jax
import jax.numpy as jnp
from jax import lax
from jax.experimental import pallas as pl
from jax.experimental.pallas import tpu as pltpu
from jax.sharding import Mesh, PartitionSpec as P

DC = 512
DR = 64
DN = 128
DV = 128
RESP = 128
PAGE = 16
LOCAL = 4
ROWS = LOCAL * RESP
EXT = 640
KEY = DC + DR
CHIPS = 16
HALF = CHIPS * PAGE
KEYS = 2 * HALF + RESP
WIDE = 2 * LOCAL * DN + EXT
OWNERS = [8 * (b & 1) + 2 * (b >> 1 & 1) + (b >> 2 & 1) for b in range(RESP // PAGE)]
SCALE = (DN + DR) ** (-0.5)
F32 = jnp.float32
BF16 = jnp.bfloat16
SAMPLE = ("xl", "y", "c")
HEAD = ("z", "xh")
PARAMS = pltpu.CompilerParams(vmem_limit_bytes=40 * 1024 * 1024)


def dot(a, b, ca, cb):
    return lax.dot_general(a, b, (((ca,), (cb,)), ((), ())), preferred_element_type=F32)


def columns(part, width):
    return slice(part * width, (part + 1) * width)


def with_rope(latent, rope):
    pad = jnp.zeros((latent.shape[0], EXT - DC - DR), BF16)
    return jnp.concatenate([latent, rope, pad], axis=1)


def pages_kernel(latent_far, rope_far, out, latent, rope, done):
    first = pltpu.make_async_copy(latent_far, latent, done.at[0])
    second = pltpu.make_async_copy(rope_far, rope, done.at[1])
    first.start()
    second.start()
    first.wait()
    second.wait()
    page = with_rope(latent[...], rope[...])
    for k in range(CHIPS):
        out[k] = page


def query_kernel(
    where,
    q_nope,
    q_rope,
    grad,
    w_key,
    w_value,
    resp_latent,
    resp_rope_t,
    query,
    d_out,
    masked_out,
    resp_keys,
):
    length = where[0]
    rope = jnp.transpose(resp_rope_t[...].astype(F32)).astype(BF16)
    resp_keys[...] = with_rope(resp_latent[...], rope)
    live = lax.broadcasted_iota(jnp.int32, (RESP, LOCAL * DV), 0) < length
    masked = jnp.where(live, grad[...].astype(F32), 0.0).astype(BF16)
    masked_out[...] = masked
    for h in range(LOCAL):
        rows = columns(h, RESP)
        latent = dot(q_nope[:, columns(h, DN)], w_key[:, columns(h, DN)], 1, 1)
        query[rows, :] = with_rope(latent.astype(BF16), q_rope[:, columns(h, DR)])
        d_out[rows, :] = dot(masked[:, columns(h, DV)], w_value[:, columns(h, DV)], 1, 1).astype(
            BF16
        )


def first_scores_kernel(where, query, d_out, own, resp_keys, scores, d_attention):
    length = where[0]
    pages = own[...].reshape(HALF, EXT)
    resp = resp_keys[...]
    scores[0:HALF, :] = dot(pages, query[...], 1, 1) * SCALE
    token = lax.broadcasted_iota(jnp.int32, (RESP, ROWS), 1) % RESP
    key_at = lax.broadcasted_iota(jnp.int32, (RESP, ROWS), 0)
    allowed = (key_at <= token) & (key_at < length)
    own_scores = dot(resp, query[...], 1, 1) * SCALE
    scores[HALF : HALF + RESP, :] = jnp.where(allowed, own_scores, -1e30)
    d_attention[0:HALF, :] = dot(pages[:, 0:DC], d_out[...], 1, 1)
    d_attention[HALF : HALF + RESP, :] = dot(resp[:, 0:DC], d_out[...], 1, 1)


def attention_kernel(
    where,
    query,
    d_out,
    own,
    other,
    resp_keys,
    first_scores,
    first_d_attention,
    attention_out,
    d_scores_out,
    keys,
):
    keys[0:HALF, :] = own[...].reshape(HALF, EXT)
    keys[HALF : 2 * HALF, :] = other[...].reshape(HALF, EXT)
    keys[2 * HALF : KEYS, :] = resp_keys[...]
    other_rows = other[...].reshape(HALF, EXT)
    other_scores = dot(other_rows, query[...], 1, 1) * SCALE
    scores = jnp.concatenate(
        [first_scores[0:HALF], other_scores, first_scores[HALF : HALF + RESP]], axis=0
    )
    highest = jnp.max(scores, axis=0, keepdims=True)
    exponent = jnp.exp(scores - highest)
    attention = exponent * (1.0 / jnp.sum(exponent, axis=0, keepdims=True))
    attention_b = attention.astype(BF16)
    attention_out[...] = attention_b
    d_attention = jnp.concatenate(
        [
            first_d_attention[0:HALF],
            dot(other_rows[:, 0:DC], d_out[...], 1, 1),
            first_d_attention[HALF : HALF + RESP],
        ],
        axis=0,
    )
    row_delta = jnp.sum(attention * d_attention, axis=0, keepdims=True)
    d_scores = (SCALE * attention * (d_attention - row_delta)).astype(BF16)
    d_scores_out[...] = d_scores


def half_grads(parity, first_key, q_nope, masked, query, d_out, attention, d_scores, d_query, out_latent, out):
    starts = [pl.multiple_of((2 * k + parity) * PAGE, PAGE) for k in range(CHIPS)]
    d_q = jnp.concatenate([d_query[pl.ds(start, PAGE), :] for start in starts], axis=0)
    values = jnp.concatenate([out_latent[pl.ds(start, PAGE), :] for start in starts], axis=0)
    for h in range(LOCAL):
        key_part = dot(d_q[:, columns(h, RESP)], q_nope[:, columns(h, DN)], 1, 0)
        out[:, :, columns(h, DN)] = key_part.astype(BF16).reshape(CHIPS, PAGE, DN)
        value_part = dot(values[:, columns(h, RESP)], masked[:, columns(h, DV)], 1, 0)
        out[:, :, columns(LOCAL + h, DN)] = value_part.astype(BF16).reshape(CHIPS, PAGE, DN)
    rows = slice(first_key, first_key + HALF)
    key_grad = dot(d_scores[rows, :], query[...], 1, 0)
    key_grad_v = dot(attention[rows, :], d_out[...], 1, 0)
    width = 2 * LOCAL * DN
    latent_part = (key_grad[:, 0:DC] + key_grad_v).astype(BF16)
    out[:, :, width : width + DC] = latent_part.reshape(CHIPS, PAGE, DC)
    out[:, :, width + DC : WIDE] = key_grad[:, DC:EXT].astype(BF16).reshape(CHIPS, PAGE, EXT - DC)


def send_kernel(
    where,
    q_nope,
    masked,
    query,
    d_out,
    keys,
    attention,
    d_scores,
    d_query,
    out_latent,
    send,
):
    d_query[...] = dot(keys[...], d_scores[...], 0, 0).astype(BF16)
    out_latent[...] = dot(keys[:, 0:DC], attention[...], 0, 0).astype(BF16)
    half_grads(1 - where[1], HALF, q_nope, masked, query, d_out, attention, d_scores, d_query, out_latent, send)


def keep_kernel(
    where,
    q_nope,
    masked,
    query,
    d_out,
    attention,
    d_scores,
    d_query,
    out_latent,
    keep,
    keep_resp,
    send_resp,
):
    half_grads(where[1], 0, q_nope, masked, query, d_out, attention, d_scores, d_query, out_latent, keep)
    own_grad = dot(d_scores[2 * HALF : KEYS, :], query[...], 1, 0)
    own_grad_v = dot(attention[2 * HALF : KEYS, :], d_out[...], 1, 0)
    resp = jnp.concatenate([own_grad[:, 0:DC] + own_grad_v, own_grad[:, DC:EXT]], axis=1)
    blocks = resp.astype(BF16).reshape(RESP // PAGE, PAGE, EXT)
    place = where[2]
    for g in range(RESP // PAGE // 2):
        low, high = blocks[g], blocks[RESP // PAGE // 2 + g]
        keep_resp[g] = jnp.where(place == 0, low, high)
        send_resp[g] = jnp.where(place == 0, high, low)


def query_grad_kernel(d_query, w_key, d_q_nope, d_q_rope):
    for h in range(LOCAL):
        d_q = d_query[0:DC, columns(h, RESP)]
        d_q_nope[:, columns(h, DN)] = dot(d_q, w_key[:, columns(h, DN)], 0, 0).astype(BF16)
    d_rope = jnp.concatenate(
        [
            jnp.transpose(d_query[DC : DC + DR, columns(h, RESP)].astype(F32)) for h in range(LOCAL)
        ],
        axis=1,
    )
    d_q_rope[...] = d_rope.astype(BF16)


def halve_kernel(bit, where, kept, received, keep, send):
    half = keep.shape[0]
    place = where[bit]
    mine = pl.ds(place * half, half)
    theirs = pl.ds((1 - place) * half, half)
    keep[...] = (kept[mine].astype(F32) + received[mine].astype(F32)).astype(BF16)
    send[...] = (kept[theirs].astype(F32) + received[theirs].astype(F32)).astype(BF16)


def line_kernel(sample_parts, kept, received, out):
    first = 2 * LOCAL * DN
    page = sample_parts[0, :, first:WIDE].astype(F32)
    for k in range(1, CHIPS):
        page = page + sample_parts[k, :, first:WIDE].astype(F32)
    rows = kept[0].astype(F32) + received[0].astype(F32)
    line = jnp.concatenate([rows[:, 0:KEY], page[:, 0:KEY]], axis=1).astype(BF16)
    for g in range(CHIPS):
        out[g] = line


def weights_kernel(sample_parts, d_key_up, d_value_up):
    for out, first in ((d_key_up, 0), (d_value_up, LOCAL * DN)):
        lanes = slice(first, first + LOCAL * DN)
        total = sample_parts[0, :, lanes].astype(F32)
        for k in range(1, CHIPS):
            total = total + sample_parts[k, :, lanes].astype(F32)
        out[...] = total


def last_kernel(parts, d_prompt, d_prompt_rope, d_resp, d_resp_rope_t):
    page = parts[0].astype(F32)
    for g in range(1, CHIPS):
        page = page + parts[g].astype(F32)
    d_prompt[...] = page[:, KEY : KEY + DC]
    d_prompt_rope[...] = page[:, KEY + DC : 2 * KEY]
    rows = jnp.concatenate(
        [parts[g, :, 0:KEY].astype(F32) + parts[g + 4, :, 0:KEY].astype(F32) for g in OWNERS],
        axis=0,
    )
    d_resp[...] = rows[:, 0:DC]
    d_resp_rope_t[...] = jnp.transpose(rows[:, DC:KEY])


def call(kernel, outs, *args, scratch=(), scalars=0, flops=0, far=False):
    vmem = pl.BlockSpec(memory_space=pltpu.VMEM)
    smem = pl.BlockSpec(memory_space=pltpu.SMEM)
    return pl.pallas_call(
        kernel,
        out_shape=[jax.ShapeDtypeStruct(shape, kind) for shape, kind in outs],
        in_specs=[smem] * scalars + [pl.BlockSpec(memory_space=pltpu.HBM) if far else vmem] * (len(args) - scalars),
        out_specs=[vmem] * len(outs),
        scratch_shapes=list(scratch),
        compiler_params=PARAMS,
        cost_estimate=pl.CostEstimate(flops=flops, bytes_accessed=0, transcendentals=0),
    )(*args)


def spread(parts, axes):
    return lax.all_to_all(parts, axes, 0, 0, tiled=True)


def body(
    q_nope,
    q_rope,
    resp_latent,
    resp_rope_t,
    prompt_latent,
    prompt_rope_t,
    w_key_up,
    w_value_up,
    grad_out,
    lengths,
):
    swap = [(0, 1), (1, 0)]
    (pages,) = call(
        pages_kernel,
        [((CHIPS, PAGE, EXT), BF16)],
        pltpu.with_memory_space_constraint(prompt_latent, pltpu.HBM),
        pltpu.with_memory_space_constraint(jnp.transpose(prompt_rope_t), pltpu.HBM),
        far=True,
        scratch=[
            pltpu.VMEM((PAGE, DC), BF16),
            pltpu.VMEM((PAGE, DR), BF16),
            pltpu.SemaphoreType.DMA((2,)),
        ],
    )
    own = spread(pages, ("xl", "y"))
    z = lax.axis_index("z")
    where = jnp.stack(
        [lengths[0], lax.axis_index("c"), z & 1, z >> 1 & 1, lax.axis_index("xh")]
    )
    query, d_out, masked, resp_keys = call(
        query_kernel,
        [
            ((ROWS, EXT), BF16),
            ((ROWS, DC), BF16),
            ((RESP, LOCAL * DV), BF16),
            ((RESP, EXT), BF16),
        ],
        where,
        q_nope,
        q_rope,
        grad_out,
        w_key_up,
        w_value_up,
        resp_latent,
        resp_rope_t,
        scalars=1,
        flops=4_000_000_000,
    )
    own, query = lax.optimization_barrier((own, query))
    other = lax.ppermute(own, "c", swap)
    first_scores, first_d_attention = call(
        first_scores_kernel,
        [((HALF + RESP, ROWS), F32)] * 2,
        where,
        query,
        d_out,
        own,
        resp_keys,
        scalars=1,
        flops=2_000_000_000,
    )
    attention, d_scores, keys = call(
        attention_kernel,
        [
            ((KEYS, ROWS), BF16),
            ((KEYS, ROWS), BF16),
            ((KEYS, EXT), BF16),
        ],
        where,
        query,
        d_out,
        own,
        other,
        resp_keys,
        first_scores,
        first_d_attention,
        scalars=1,
        flops=4_000_000_000,
    )
    d_query, out_latent, send = call(
        send_kernel,
        [
            ((EXT, ROWS), BF16),
            ((DC, ROWS), BF16),
            ((CHIPS, PAGE, WIDE), BF16),
        ],
        where,
        q_nope,
        masked,
        query,
        d_out,
        keys,
        attention,
        d_scores,
        scalars=1,
        flops=4_000_000_000,
    )
    keep, keep_resp, send_resp = call(
        keep_kernel,
        [
            ((CHIPS, PAGE, WIDE), BF16),
            ((RESP // PAGE // 2, PAGE, EXT), BF16),
            ((RESP // PAGE // 2, PAGE, EXT), BF16),
        ],
        where,
        q_nope,
        masked,
        query,
        d_out,
        attention,
        d_scores,
        d_query,
        out_latent,
        scalars=1,
        flops=2_000_000_000,
    )
    got_resp = lax.ppermute(send_resp, "z", [(i, i ^ 1) for i in range(8)])
    chip_sum = keep + lax.ppermute(send, "c", swap)
    sample_parts = spread(chip_sum, ("xl", "y"))
    d_q_nope, d_q_rope = call(
        query_grad_kernel,
        [((RESP, LOCAL * DN), BF16), ((RESP, LOCAL * DR), BF16)],
        d_query,
        w_key_up,
        flops=1_000_000_000,
    )
    keep_resp, send_resp = call(
        functools.partial(halve_kernel, 3),
        [((2, PAGE, EXT), BF16)] * 2,
        where,
        keep_resp,
        got_resp,
        scalars=1,
    )
    got_resp = lax.ppermute(send_resp, "z", [(i, i ^ 2) for i in range(8)])
    keep_resp, send_resp = call(
        functools.partial(halve_kernel, 4),
        [((1, PAGE, EXT), BF16)] * 2,
        where,
        keep_resp,
        got_resp,
        scalars=1,
    )
    got_resp = lax.ppermute(send_resp, "xh", swap)
    (line,) = call(
        line_kernel,
        [((CHIPS, PAGE, 2 * KEY), BF16)],
        sample_parts,
        keep_resp,
        got_resp,
    )
    d_key_up, d_value_up = call(
        weights_kernel,
        [((PAGE, LOCAL * DN), F32), ((PAGE, LOCAL * DV), F32)],
        sample_parts,
        flops=1_000_000_000,
    )
    lines = spread(line, ("xh", "z"))
    d_prompt, d_prompt_rope, d_resp, d_resp_rope_t = call(
        last_kernel,
        [
            ((PAGE, DC), F32),
            ((PAGE, DR), F32),
            ((RESP, DC), F32),
            ((DR, RESP), F32),
        ],
        lines,
    )
    return (
        d_q_nope,
        d_q_rope,
        d_key_up,
        d_value_up,
        d_prompt,
        jnp.transpose(d_prompt_rope),
        d_resp,
        d_resp_rope_t,
    )


def solution(mesh):
    fine = Mesh(mesh.devices.reshape(2, 8, 2, 8, 2), SAMPLE + HEAD)
    return jax.shard_map(
        body,
        mesh=fine,
        in_specs=(
            P(SAMPLE, HEAD),
            P(SAMPLE, HEAD),
            P(SAMPLE, None),
            P(None, SAMPLE),
            P(SAMPLE, None),
            P(None, SAMPLE),
            P(None, HEAD),
            P(None, HEAD),
            P(SAMPLE, HEAD),
            P(SAMPLE),
        ),
        out_specs=(
            P(SAMPLE, HEAD),
            P(SAMPLE, HEAD),
            P(SAMPLE, HEAD),
            P(SAMPLE, HEAD),
            P(SAMPLE, None),
            P(None, SAMPLE),
            P(SAMPLE, None),
            P(None, SAMPLE),
        ),
        check_vma=False,
    )
```

```python
import functools

import jax
import jax.numpy as jnp
from jax import lax
from jax.experimental import pallas as pl
from jax.experimental.pallas import tpu as pltpu
from jax.sharding import Mesh, PartitionSpec as P

DC = 512
DR = 64
DN = 128
DV = 128
RESP = 128
PAGE = 16
LOCAL = 4
ROWS = LOCAL * RESP
EXT = 640
KEY = DC + DR
CHIPS = 16
HALF = CHIPS * PAGE
KEYS = 2 * HALF + RESP
ROPE_AT = (2 * LOCAL + DC // 128) * PAGE
WIDE = ROPE_AT + 8
OWNERS = [8 * (b & 1) + 2 * (b >> 1 & 1) + (b >> 2 & 1) for b in range(RESP // PAGE)]
SCALE = (DN + DR) ** (-0.5)
F32 = jnp.float32
BF16 = jnp.bfloat16
SAMPLE = ("xl", "y", "c")
HEAD = ("z", "xh")
PARAMS = pltpu.CompilerParams(vmem_limit_bytes=40 * 1024 * 1024)


def dot(a, b, ca, cb):
    return lax.dot_general(a, b, (((ca,), (cb,)), ((), ())), preferred_element_type=F32)


def columns(part, width):
    return slice(part * width, (part + 1) * width)


def with_rope(latent, rope):
    pad = jnp.zeros((latent.shape[0], EXT - DC - DR), BF16)
    return jnp.concatenate([latent, rope, pad], axis=1)


def pages_kernel(latent_far, rope_far, out, latent, rope, done):
    first = pltpu.make_async_copy(latent_far, latent, done.at[0])
    second = pltpu.make_async_copy(rope_far, rope, done.at[1])
    first.start()
    second.start()
    first.wait()
    second.wait()
    page = with_rope(latent[...], rope[...])
    for k in range(CHIPS):
        out[k] = page


def query_kernel(
    where,
    q_nope,
    q_rope,
    grad,
    w_key,
    w_value,
    resp_latent,
    resp_rope_t,
    query,
    d_out,
    masked_out,
    resp_keys,
):
    length = where[0]
    rope = jnp.transpose(resp_rope_t[...].astype(F32)).astype(BF16)
    resp_keys[...] = with_rope(resp_latent[...], rope)
    live = lax.broadcasted_iota(jnp.int32, (RESP, LOCAL * DV), 0) < length
    masked = jnp.where(live, grad[...].astype(F32), 0.0).astype(BF16)
    masked_out[...] = masked
    for h in range(LOCAL):
        rows = columns(h, RESP)
        latent = dot(q_nope[:, columns(h, DN)], w_key[:, columns(h, DN)], 1, 1)
        query[rows, :] = with_rope(latent.astype(BF16), q_rope[:, columns(h, DR)])
        d_out[rows, :] = dot(masked[:, columns(h, DV)], w_value[:, columns(h, DV)], 1, 1).astype(
            BF16
        )


def first_scores_kernel(where, query, d_out, own, resp_keys, scores, d_attention):
    length = where[0]
    pages = own[...].reshape(HALF, EXT)
    resp = resp_keys[...]
    scores[0:HALF, :] = dot(pages, query[...], 1, 1) * SCALE
    token = lax.broadcasted_iota(jnp.int32, (RESP, ROWS), 1) % RESP
    key_at = lax.broadcasted_iota(jnp.int32, (RESP, ROWS), 0)
    allowed = (key_at <= token) & (key_at < length)
    own_scores = dot(resp, query[...], 1, 1) * SCALE
    scores[HALF : HALF + RESP, :] = jnp.where(allowed, own_scores, -1e30)
    d_attention[0:HALF, :] = dot(pages[:, 0:DC], d_out[...], 1, 1)
    d_attention[HALF : HALF + RESP, :] = dot(resp[:, 0:DC], d_out[...], 1, 1)


def attention_kernel(
    where,
    q_nope,
    masked,
    query,
    d_out,
    own,
    other,
    resp_keys,
    first_scores,
    first_d_attention,
    attention_out,
    d_scores_out,
    d_query,
    out_latent,
    send,
    keys,
):
    keys[0:HALF, :] = own[...].reshape(HALF, EXT)
    keys[HALF : 2 * HALF, :] = other[...].reshape(HALF, EXT)
    keys[2 * HALF : KEYS, :] = resp_keys[...]
    other_rows = other[...].reshape(HALF, EXT)
    other_scores = dot(other_rows, query[...], 1, 1) * SCALE
    scores = jnp.concatenate(
        [first_scores[0:HALF], other_scores, first_scores[HALF : HALF + RESP]], axis=0
    )
    highest = jnp.max(scores, axis=0, keepdims=True)
    exponent = jnp.exp(scores - highest)
    attention = exponent * (1.0 / jnp.sum(exponent, axis=0, keepdims=True))
    attention_b = attention.astype(BF16)
    attention_out[...] = attention_b
    d_attention = jnp.concatenate(
        [
            first_d_attention[0:HALF],
            dot(other_rows[:, 0:DC], d_out[...], 1, 1),
            first_d_attention[HALF : HALF + RESP],
        ],
        axis=0,
    )
    row_delta = jnp.sum(attention * d_attention, axis=0, keepdims=True)
    d_scores = (SCALE * attention * (d_attention - row_delta)).astype(BF16)
    d_scores_out[...] = d_scores
    d_query[...] = dot(keys[...], d_scores, 0, 0).astype(BF16)
    out_latent[...] = dot(keys[:, 0:DC], attention_b, 0, 0).astype(BF16)
    half_grads(
        1 - where[1],
        HALF,
        q_nope,
        masked,
        query,
        d_out,
        attention_out,
        d_scores_out,
        d_query,
        out_latent,
        send,
    )


def half_grads(parity, first_key, q_nope, masked, query, d_out, attention, d_scores, d_query, out_latent, out):
    starts = [pl.multiple_of((2 * k + parity) * PAGE, PAGE) for k in range(CHIPS)]
    d_q = jnp.concatenate([d_query[pl.ds(start, PAGE), :] for start in starts], axis=0)
    values = jnp.concatenate([out_latent[pl.ds(start, PAGE), :] for start in starts], axis=0)
    blocks = []
    for h in range(LOCAL):
        blocks.append(dot(d_q[:, columns(h, RESP)], q_nope[:, columns(h, DN)], 1, 0))
    for h in range(LOCAL):
        blocks.append(dot(values[:, columns(h, RESP)], masked[:, columns(h, DV)], 1, 0))
    rows = slice(first_key, first_key + HALF)
    key_grad = dot(d_scores[rows, :], query[...], 1, 0)
    latent_part = key_grad[:, 0:DC] + dot(attention[rows, :], d_out[...], 1, 0)
    blocks += [latent_part[:, columns(part, 128)] for part in range(DC // 128)]
    for at, block in enumerate(blocks):
        out[:, columns(at, PAGE), :] = block.astype(BF16).reshape(CHIPS, PAGE, 128)
    rope = key_grad[:, DC : DC + DR].reshape(CHIPS, PAGE, DR)
    rope = jnp.concatenate([rope[:, 0:8], rope[:, 8:16]], axis=2)
    out[:, ROPE_AT:WIDE, :] = rope.astype(BF16)


def keep_kernel(
    where,
    q_nope,
    masked,
    query,
    d_out,
    attention,
    d_scores,
    d_query,
    out_latent,
    keep,
    keep_resp,
    send_resp,
):
    half_grads(where[1], 0, q_nope, masked, query, d_out, attention, d_scores, d_query, out_latent, keep)
    own_grad = dot(d_scores[2 * HALF : KEYS, :], query[...], 1, 0)
    own_grad_v = dot(attention[2 * HALF : KEYS, :], d_out[...], 1, 0)
    resp = jnp.concatenate([own_grad[:, 0:DC] + own_grad_v, own_grad[:, DC:EXT]], axis=1)
    blocks = resp.astype(BF16).reshape(RESP // PAGE, PAGE, EXT)
    place = where[2]
    for g in range(RESP // PAGE // 2):
        low, high = blocks[g], blocks[RESP // PAGE // 2 + g]
        keep_resp[g] = jnp.where(place == 0, low, high)
        send_resp[g] = jnp.where(place == 0, high, low)


def query_grad_kernel(d_query, w_key, d_q_nope, d_q_rope):
    for h in range(LOCAL):
        d_q = d_query[0:DC, columns(h, RESP)]
        d_q_nope[:, columns(h, DN)] = dot(d_q, w_key[:, columns(h, DN)], 0, 0).astype(BF16)
    d_rope = jnp.concatenate(
        [
            jnp.transpose(d_query[DC : DC + DR, columns(h, RESP)].astype(F32)) for h in range(LOCAL)
        ],
        axis=1,
    )
    d_q_rope[...] = d_rope.astype(BF16)


def halve_kernel(bit, where, kept, received, keep, send):
    half = keep.shape[0]
    place = where[bit]
    mine = pl.ds(place * half, half)
    theirs = pl.ds((1 - place) * half, half)
    keep[...] = (kept[mine].astype(F32) + received[mine].astype(F32)).astype(BF16)
    send[...] = (kept[theirs].astype(F32) + received[theirs].astype(F32)).astype(BF16)


def add_blocks(parts, rows):
    total = parts[0, rows, :].astype(F32)
    for k in range(1, CHIPS):
        total = total + parts[k, rows, :].astype(F32)
    return total


def line_kernel(sample_parts, kept, received, out):
    latent = add_blocks(sample_parts, slice(2 * LOCAL * PAGE, ROPE_AT))
    rope = add_blocks(sample_parts, slice(ROPE_AT, WIDE))
    rope = jnp.concatenate([rope[:, 0:DR], rope[:, DR : 2 * DR]], axis=0)
    rows = kept[0].astype(F32) + received[0].astype(F32)
    line = jnp.concatenate(
        [rows[:, 0:KEY]] + [latent[columns(part, PAGE)] for part in range(DC // 128)] + [rope],
        axis=1,
    ).astype(BF16)
    for g in range(CHIPS):
        out[g] = line


def weights_kernel(sample_parts, d_key_up, d_value_up):
    total = add_blocks(sample_parts, slice(0, 2 * LOCAL * PAGE))
    for h in range(LOCAL):
        d_key_up[:, columns(h, DN)] = total[columns(h, PAGE)]
        d_value_up[:, columns(h, DV)] = total[columns(LOCAL + h, PAGE)]


def last_kernel(parts, d_prompt, d_prompt_rope, d_resp, d_resp_rope_t):
    page = parts[0].astype(F32)
    for g in range(1, CHIPS):
        page = page + parts[g].astype(F32)
    d_prompt[...] = page[:, KEY : KEY + DC]
    d_prompt_rope[...] = page[:, KEY + DC : 2 * KEY]
    rows = jnp.concatenate(
        [parts[g, :, 0:KEY].astype(F32) + parts[g + 4, :, 0:KEY].astype(F32) for g in OWNERS],
        axis=0,
    )
    d_resp[...] = rows[:, 0:DC]
    d_resp_rope_t[...] = jnp.transpose(rows[:, DC:KEY])


def call(kernel, outs, *args, scratch=(), scalars=0, flops=0, far=False):
    vmem = pl.BlockSpec(memory_space=pltpu.VMEM)
    smem = pl.BlockSpec(memory_space=pltpu.SMEM)
    return pl.pallas_call(
        kernel,
        out_shape=[jax.ShapeDtypeStruct(shape, kind) for shape, kind in outs],
        in_specs=[smem] * scalars + [pl.BlockSpec(memory_space=pltpu.HBM) if far else vmem] * (len(args) - scalars),
        out_specs=[vmem] * len(outs),
        scratch_shapes=list(scratch),
        compiler_params=PARAMS,
        cost_estimate=pl.CostEstimate(flops=flops, bytes_accessed=0, transcendentals=0),
    )(*args)


def spread(parts, axes):
    return lax.all_to_all(parts, axes, 0, 0, tiled=True)


def body(
    q_nope,
    q_rope,
    resp_latent,
    resp_rope_t,
    prompt_latent,
    prompt_rope_t,
    w_key_up,
    w_value_up,
    grad_out,
    lengths,
):
    swap = [(0, 1), (1, 0)]
    (pages,) = call(
        pages_kernel,
        [((CHIPS, PAGE, EXT), BF16)],
        pltpu.with_memory_space_constraint(prompt_latent, pltpu.HBM),
        pltpu.with_memory_space_constraint(jnp.transpose(prompt_rope_t), pltpu.HBM),
        far=True,
        scratch=[
            pltpu.VMEM((PAGE, DC), BF16),
            pltpu.VMEM((PAGE, DR), BF16),
            pltpu.SemaphoreType.DMA((2,)),
        ],
    )
    own = spread(pages, ("xl", "y"))
    z = lax.axis_index("z")
    where = jnp.stack(
        [lengths[0], lax.axis_index("c"), z & 1, z >> 1 & 1, lax.axis_index("xh")]
    )
    query, d_out, masked, resp_keys = call(
        query_kernel,
        [
            ((ROWS, EXT), BF16),
            ((ROWS, DC), BF16),
            ((RESP, LOCAL * DV), BF16),
            ((RESP, EXT), BF16),
        ],
        where,
        q_nope,
        q_rope,
        grad_out,
        w_key_up,
        w_value_up,
        resp_latent,
        resp_rope_t,
        scalars=1,
        flops=4_000_000_000,
    )
    own, query = lax.optimization_barrier((own, query))
    other = lax.ppermute(own, "c", swap)
    first_scores, first_d_attention = call(
        first_scores_kernel,
        [((HALF + RESP, ROWS), F32)] * 2,
        where,
        query,
        d_out,
        own,
        resp_keys,
        scalars=1,
        flops=2_000_000_000,
    )
    attention, d_scores, d_query, out_latent, send = call(
        attention_kernel,
        [
            ((KEYS, ROWS), BF16),
            ((KEYS, ROWS), BF16),
            ((EXT, ROWS), BF16),
            ((DC, ROWS), BF16),
            ((CHIPS, WIDE, 128), BF16),
        ],
        where,
        q_nope,
        masked,
        query,
        d_out,
        own,
        other,
        resp_keys,
        first_scores,
        first_d_attention,
        scalars=1,
        flops=4_000_000_000,
        scratch=[pltpu.VMEM((KEYS, EXT), BF16)],
    )
    keep, keep_resp, send_resp = call(
        keep_kernel,
        [
            ((CHIPS, WIDE, 128), BF16),
            ((RESP // PAGE // 2, PAGE, EXT), BF16),
            ((RESP // PAGE // 2, PAGE, EXT), BF16),
        ],
        where,
        q_nope,
        masked,
        query,
        d_out,
        attention,
        d_scores,
        d_query,
        out_latent,
        scalars=1,
        flops=2_000_000_000,
    )
    got_resp = lax.ppermute(send_resp, "z", [(i, i ^ 1) for i in range(8)])
    chip_sum = keep + lax.ppermute(send, "c", swap)
    sample_parts = spread(chip_sum, ("xl", "y"))
    d_q_nope, d_q_rope = call(
        query_grad_kernel,
        [((RESP, LOCAL * DN), BF16), ((RESP, LOCAL * DR), BF16)],
        d_query,
        w_key_up,
        flops=1_000_000_000,
    )
    keep_resp, send_resp = call(
        functools.partial(halve_kernel, 3),
        [((2, PAGE, EXT), BF16)] * 2,
        where,
        keep_resp,
        got_resp,
        scalars=1,
    )
    got_resp = lax.ppermute(send_resp, "z", [(i, i ^ 2) for i in range(8)])
    keep_resp, send_resp = call(
        functools.partial(halve_kernel, 4),
        [((1, PAGE, EXT), BF16)] * 2,
        where,
        keep_resp,
        got_resp,
        scalars=1,
    )
    got_resp = lax.ppermute(send_resp, "xh", swap)
    (line,) = call(
        line_kernel,
        [((CHIPS, PAGE, 2 * KEY), BF16)],
        sample_parts,
        keep_resp,
        got_resp,
    )
    d_key_up, d_value_up = call(
        weights_kernel,
        [((PAGE, LOCAL * DN), F32), ((PAGE, LOCAL * DV), F32)],
        sample_parts,
        flops=1_000_000_000,
    )
    lines = spread(line, ("xh", "z"))
    d_prompt, d_prompt_rope, d_resp, d_resp_rope_t = call(
        last_kernel,
        [
            ((PAGE, DC), F32),
            ((PAGE, DR), F32),
            ((RESP, DC), F32),
            ((DR, RESP), F32),
        ],
        lines,
    )
    return (
        d_q_nope,
        d_q_rope,
        d_key_up,
        d_value_up,
        d_prompt,
        jnp.transpose(d_prompt_rope),
        d_resp,
        d_resp_rope_t,
    )


def solution(mesh):
    fine = Mesh(mesh.devices.reshape(2, 8, 2, 8, 2), SAMPLE + HEAD)
    return jax.shard_map(
        body,
        mesh=fine,
        in_specs=(
            P(SAMPLE, HEAD),
            P(SAMPLE, HEAD),
            P(SAMPLE, None),
            P(None, SAMPLE),
            P(SAMPLE, None),
            P(None, SAMPLE),
            P(None, HEAD),
            P(None, HEAD),
            P(SAMPLE, HEAD),
            P(SAMPLE),
        ),
        out_specs=(
            P(SAMPLE, HEAD),
            P(SAMPLE, HEAD),
            P(SAMPLE, HEAD),
            P(SAMPLE, HEAD),
            P(SAMPLE, None),
            P(None, SAMPLE),
            P(SAMPLE, None),
            P(None, SAMPLE),
        ),
        check_vma=False,
    )
```

```python
import functools

import jax
import jax.numpy as jnp
from jax import lax
from jax.experimental import pallas as pl
from jax.experimental.pallas import tpu as pltpu
from jax.sharding import Mesh, PartitionSpec as P

DC = 512
DR = 64
DN = 128
DV = 128
RESP = 128
PAGE = 16
LOCAL = 4
ROWS = LOCAL * RESP
EXT = 640
KEY = DC + DR
CHIPS = 16
HALF = CHIPS * PAGE
KEYS = 2 * HALF + RESP
ROPE_AT = (2 * LOCAL + DC // 128) * PAGE
WIDE = ROPE_AT + 8
PACKED = DC // 128 * PAGE + 8
OWNERS = [8 * (b & 1) + (3, 0, 1, 2)[b >> 1] for b in range(RESP // PAGE)]
SCALE = (DN + DR) ** (-0.5)
F32 = jnp.float32
BF16 = jnp.bfloat16
SAMPLE = ("xl", "y", "c")
HEAD = ("z", "xh")
PARAMS = pltpu.CompilerParams(vmem_limit_bytes=40 * 1024 * 1024)


def dot(a, b, ca, cb):
    return lax.dot_general(a, b, (((ca,), (cb,)), ((), ())), preferred_element_type=F32)


def columns(part, width):
    return slice(part * width, (part + 1) * width)


def with_rope(latent, rope):
    pad = jnp.zeros((latent.shape[0], EXT - DC - DR), BF16)
    return jnp.concatenate([latent, rope, pad], axis=1)


def pages_kernel(latent_far, rope_far, out, latent, rope, done):
    first = pltpu.make_async_copy(latent_far, latent, done.at[0])
    second = pltpu.make_async_copy(rope_far, rope, done.at[1])
    first.start()
    second.start()
    first.wait()
    second.wait()
    rows = rope[...].astype(F32)
    rows = jnp.concatenate([rows[0:8], rows[8:16]], axis=1).astype(BF16)
    for k in range(CHIPS):
        for part in range(DC // 128):
            out[k, columns(part, PAGE), :] = latent[:, columns(part, 128)]
        out[k, DC // 128 * PAGE : PACKED, :] = rows


def unpack(pages, keys):
    for part in range(DC // 128):
        block = pages[:, columns(part, PAGE), :]
        keys[:, columns(part, 128)] = block.reshape(HALF, 128)
    rope = pages[:, DC // 128 * PAGE : PACKED, :].astype(F32)
    rope = jnp.concatenate([rope[:, :, 0:DR], rope[:, :, DR : 2 * DR]], axis=1)
    rope = jnp.concatenate([rope, jnp.zeros_like(rope)], axis=2)
    keys[:, DC:EXT] = rope.reshape(HALF, EXT - DC).astype(BF16)


def query_kernel(
    where,
    q_nope,
    q_rope,
    grad,
    w_key,
    w_value,
    resp_latent,
    resp_rope_t,
    query,
    d_out,
    masked_out,
    resp_keys,
):
    length = where[0]
    rope = jnp.transpose(resp_rope_t[...].astype(F32)).astype(BF16)
    resp_keys[...] = with_rope(resp_latent[...], rope)
    live = lax.broadcasted_iota(jnp.int32, (RESP, LOCAL * DV), 0) < length
    masked = jnp.where(live, grad[...].astype(F32), 0.0).astype(BF16)
    masked_out[...] = masked
    for h in range(LOCAL):
        rows = columns(h, RESP)
        latent = dot(q_nope[:, columns(h, DN)], w_key[:, columns(h, DN)], 1, 1)
        query[rows, :] = with_rope(latent.astype(BF16), q_rope[:, columns(h, DR)])
        d_out[rows, :] = dot(masked[:, columns(h, DV)], w_value[:, columns(h, DV)], 1, 1).astype(
            BF16
        )


def first_scores_kernel(where, query, d_out, own, resp_keys, scores, d_attention, own_keys):
    length = where[0]
    unpack(own, own_keys)
    pages = own_keys[...]
    resp = resp_keys[...]
    scores[0:HALF, :] = dot(pages, query[...], 1, 1) * SCALE
    token = lax.broadcasted_iota(jnp.int32, (RESP, ROWS), 1) % RESP
    key_at = lax.broadcasted_iota(jnp.int32, (RESP, ROWS), 0)
    allowed = (key_at <= token) & (key_at < length)
    own_scores = dot(resp, query[...], 1, 1) * SCALE
    scores[HALF : HALF + RESP, :] = jnp.where(allowed, own_scores, -1e30)
    d_attention[0:HALF, :] = dot(pages[:, 0:DC], d_out[...], 1, 1)
    d_attention[HALF : HALF + RESP, :] = dot(resp[:, 0:DC], d_out[...], 1, 1)


def attention_kernel(
    where,
    q_nope,
    masked,
    query,
    d_out,
    own,
    other,
    resp_keys,
    first_scores,
    first_d_attention,
    attention_out,
    d_scores_out,
    d_query,
    out_latent,
    send,
    keys,
):
    keys[0:HALF, :] = own[...]
    unpack(other, keys.at[HALF : 2 * HALF])
    keys[2 * HALF : KEYS, :] = resp_keys[...]
    other_rows = keys[HALF : 2 * HALF, :]
    other_scores = dot(other_rows, query[...], 1, 1) * SCALE
    scores = jnp.concatenate(
        [first_scores[0:HALF], other_scores, first_scores[HALF : HALF + RESP]], axis=0
    )
    highest = jnp.max(scores, axis=0, keepdims=True)
    exponent = jnp.exp(scores - highest)
    attention = exponent * (1.0 / jnp.sum(exponent, axis=0, keepdims=True))
    attention_b = attention.astype(BF16)
    attention_out[...] = attention_b
    d_attention = jnp.concatenate(
        [
            first_d_attention[0:HALF],
            dot(other_rows[:, 0:DC], d_out[...], 1, 1),
            first_d_attention[HALF : HALF + RESP],
        ],
        axis=0,
    )
    row_delta = jnp.sum(attention * d_attention, axis=0, keepdims=True)
    d_scores = (SCALE * attention * (d_attention - row_delta)).astype(BF16)
    d_scores_out[...] = d_scores
    d_query[...] = dot(keys[...], d_scores, 0, 0).astype(BF16)
    out_latent[...] = dot(keys[:, 0:DC], attention_b, 0, 0).astype(BF16)
    half_grads(
        1 - where[1],
        HALF,
        q_nope,
        masked,
        query,
        d_out,
        attention_out,
        d_scores_out,
        d_query,
        out_latent,
        send,
    )


def half_grads(parity, first_key, q_nope, masked, query, d_out, attention, d_scores, d_query, out_latent, out):
    starts = [pl.multiple_of((2 * k + parity) * PAGE, PAGE) for k in range(CHIPS)]
    d_q = jnp.concatenate([d_query[pl.ds(start, PAGE), :] for start in starts], axis=0)
    values = jnp.concatenate([out_latent[pl.ds(start, PAGE), :] for start in starts], axis=0)
    blocks = []
    for h in range(LOCAL):
        blocks.append(dot(d_q[:, columns(h, RESP)], q_nope[:, columns(h, DN)], 1, 0))
    for h in range(LOCAL):
        blocks.append(dot(values[:, columns(h, RESP)], masked[:, columns(h, DV)], 1, 0))
    rows = slice(first_key, first_key + HALF)
    key_grad = dot(d_scores[rows, :], query[...], 1, 0)
    latent_part = key_grad[:, 0:DC] + dot(attention[rows, :], d_out[...], 1, 0)
    blocks += [latent_part[:, columns(part, 128)] for part in range(DC // 128)]
    for at, block in enumerate(blocks):
        out[:, columns(at, PAGE), :] = block.astype(BF16).reshape(CHIPS, PAGE, 128)
    rope = key_grad[:, DC : DC + DR].reshape(CHIPS, PAGE, DR)
    rope = jnp.concatenate([rope[:, 0:8], rope[:, 8:16]], axis=2)
    out[:, ROPE_AT:WIDE, :] = rope.astype(BF16)


def keep_kernel(
    where,
    q_nope,
    masked,
    query,
    d_out,
    attention,
    d_scores,
    d_query,
    out_latent,
    keep,
    keep_resp,
    send_resp,
):
    half_grads(where[1], 0, q_nope, masked, query, d_out, attention, d_scores, d_query, out_latent, keep)
    own_grad = dot(d_scores[2 * HALF : KEYS, :], query[...], 1, 0)
    own_grad_v = dot(attention[2 * HALF : KEYS, :], d_out[...], 1, 0)
    latent = (own_grad[:, 0:DC] + own_grad_v).reshape(RESP // PAGE, PAGE, DC)
    rope = own_grad[:, DC:KEY].reshape(RESP // PAGE, PAGE, DR)
    packed = jnp.concatenate(
        [latent[:, :, columns(part, 128)] for part in range(DC // 128)]
        + [jnp.concatenate([rope[:, 0:8], rope[:, 8:16]], axis=2)],
        axis=1,
    ).astype(BF16)
    place = where[2]
    for g in range(RESP // PAGE // 2):
        low, high = packed[g], packed[RESP // PAGE // 2 + g]
        keep_resp[g] = jnp.where(place == 0, low, high)
        send_resp[g] = jnp.where(place == 0, high, low)


def query_grad_kernel(d_query, w_key, d_q_nope, d_q_rope):
    for h in range(LOCAL):
        d_q = d_query[0:DC, columns(h, RESP)]
        d_q_nope[:, columns(h, DN)] = dot(d_q, w_key[:, columns(h, DN)], 0, 0).astype(BF16)
    d_rope = jnp.concatenate(
        [
            jnp.transpose(d_query[DC : DC + DR, columns(h, RESP)].astype(F32)) for h in range(LOCAL)
        ],
        axis=1,
    )
    d_q_rope[...] = d_rope.astype(BF16)


def halve_kernel(bit, where, kept, received, keep, send):
    half = keep.shape[0]
    place = where[bit]
    mine = pl.ds(place * half, half)
    theirs = pl.ds((1 - place) * half, half)
    keep[...] = (kept[mine].astype(F32) + received[mine].astype(F32)).astype(BF16)
    send[...] = (kept[theirs].astype(F32) + received[theirs].astype(F32)).astype(BF16)


def add_blocks(parts, rows):
    total = parts[0, rows, :].astype(F32)
    for k in range(1, CHIPS):
        total = total + parts[k, rows, :].astype(F32)
    return total


def line_kernel(sample_parts, kept, received, out):
    page = add_blocks(sample_parts, slice(2 * LOCAL * PAGE, WIDE))
    rows = kept[0].astype(F32) + received[0].astype(F32)
    line = jnp.concatenate([rows, page], axis=0).astype(BF16)
    for g in range(CHIPS):
        out[g] = line


def weights_kernel(sample_parts, d_key_up, d_value_up):
    total = add_blocks(sample_parts, slice(0, 2 * LOCAL * PAGE))
    for h in range(LOCAL):
        d_key_up[:, columns(h, DN)] = total[columns(h, PAGE)]
        d_value_up[:, columns(h, DV)] = total[columns(LOCAL + h, PAGE)]


def unpacked(block):
    latent = [block[columns(part, PAGE)] for part in range(DC // 128)]
    rope = block[DC // 128 * PAGE : PACKED]
    return (
        jnp.concatenate(latent, axis=1),
        jnp.concatenate([rope[:, 0:DR], rope[:, DR : 2 * DR]], axis=0),
    )


def last_kernel(parts, d_prompt, d_prompt_rope, d_resp, d_resp_rope_t):
    latent, rope = unpacked(add_blocks(parts, slice(PACKED, 2 * PACKED)))
    d_prompt[...] = latent
    d_prompt_rope[...] = rope
    ropes = []
    for at, g in enumerate(OWNERS):
        block = parts[g, 0:PACKED, :].astype(F32) + parts[g + 4, 0:PACKED, :].astype(F32)
        latent, rope = unpacked(block)
        d_resp[columns(at, PAGE), :] = latent
        ropes.append(rope)
    d_resp_rope_t[...] = jnp.transpose(jnp.concatenate(ropes, axis=0))


def call(kernel, outs, *args, scratch=(), scalars=0, flops=0, far=False):
    vmem = pl.BlockSpec(memory_space=pltpu.VMEM)
    smem = pl.BlockSpec(memory_space=pltpu.SMEM)
    return pl.pallas_call(
        kernel,
        out_shape=[jax.ShapeDtypeStruct(shape, kind) for shape, kind in outs],
        in_specs=[smem] * scalars + [pl.BlockSpec(memory_space=pltpu.HBM) if far else vmem] * (len(args) - scalars),
        out_specs=[vmem] * len(outs),
        scratch_shapes=list(scratch),
        compiler_params=PARAMS,
        cost_estimate=pl.CostEstimate(flops=flops, bytes_accessed=0, transcendentals=0),
    )(*args)


def spread(parts, axes):
    return lax.all_to_all(parts, axes, 0, 0, tiled=True)


def body(
    q_nope,
    q_rope,
    resp_latent,
    resp_rope_t,
    prompt_latent,
    prompt_rope_t,
    w_key_up,
    w_value_up,
    grad_out,
    lengths,
):
    swap = [(0, 1), (1, 0)]
    (pages,) = call(
        pages_kernel,
        [((CHIPS, PACKED, 128), BF16)],
        pltpu.with_memory_space_constraint(prompt_latent, pltpu.HBM),
        pltpu.with_memory_space_constraint(jnp.transpose(prompt_rope_t), pltpu.HBM),
        far=True,
        scratch=[
            pltpu.VMEM((PAGE, DC), BF16),
            pltpu.VMEM((PAGE, DR), BF16),
            pltpu.SemaphoreType.DMA((2,)),
        ],
    )
    own = spread(pages, ("xl", "y"))
    z = lax.axis_index("z")
    where = jnp.stack(
        [lengths[0], lax.axis_index("c"), (z + 1) >> 1 & 1, 1 - (z & 1), lax.axis_index("xh")]
    )
    query, d_out, masked, resp_keys = call(
        query_kernel,
        [
            ((ROWS, EXT), BF16),
            ((ROWS, DC), BF16),
            ((RESP, LOCAL * DV), BF16),
            ((RESP, EXT), BF16),
        ],
        where,
        q_nope,
        q_rope,
        grad_out,
        w_key_up,
        w_value_up,
        resp_latent,
        resp_rope_t,
        scalars=1,
        flops=4_000_000_000,
    )
    own, query = lax.optimization_barrier((own, query))
    other = lax.ppermute(own, "c", swap)
    first_scores, first_d_attention, own_keys = call(
        first_scores_kernel,
        [((HALF + RESP, ROWS), F32)] * 2 + [((HALF, EXT), BF16)],
        where,
        query,
        d_out,
        own,
        resp_keys,
        scalars=1,
        flops=2_000_000_000,
    )
    attention, d_scores, d_query, out_latent, send = call(
        attention_kernel,
        [
            ((KEYS, ROWS), BF16),
            ((KEYS, ROWS), BF16),
            ((EXT, ROWS), BF16),
            ((DC, ROWS), BF16),
            ((CHIPS, WIDE, 128), BF16),
        ],
        where,
        q_nope,
        masked,
        query,
        d_out,
        own_keys,
        other,
        resp_keys,
        first_scores,
        first_d_attention,
        scalars=1,
        flops=4_000_000_000,
        scratch=[pltpu.VMEM((KEYS, EXT), BF16)],
    )
    keep, keep_resp, send_resp = call(
        keep_kernel,
        [
            ((CHIPS, WIDE, 128), BF16),
            ((RESP // PAGE // 2, PACKED, 128), BF16),
            ((RESP // PAGE // 2, PACKED, 128), BF16),
        ],
        where,
        q_nope,
        masked,
        query,
        d_out,
        attention,
        d_scores,
        d_query,
        out_latent,
        scalars=1,
        flops=2_000_000_000,
    )
    got_resp = lax.ppermute(send_resp, "z", [(i, i ^ 1) for i in range(8)])
    chip_sum = keep + lax.ppermute(send, "c", swap)
    sample_parts = spread(chip_sum, ("xl", "y"))
    d_q_nope, d_q_rope = call(
        query_grad_kernel,
        [((RESP, LOCAL * DN), BF16), ((RESP, LOCAL * DR), BF16)],
        d_query,
        w_key_up,
        flops=1_000_000_000,
    )
    keep_resp, send_resp = call(
        functools.partial(halve_kernel, 3),
        [((2, PACKED, 128), BF16)] * 2,
        where,
        keep_resp,
        got_resp,
        scalars=1,
    )
    got_resp = lax.ppermute(send_resp, "z", [(i, (i + 2 * (i & 1) - 1) % 8) for i in range(8)])
    keep_resp, send_resp = call(
        functools.partial(halve_kernel, 4),
        [((1, PACKED, 128), BF16)] * 2,
        where,
        keep_resp,
        got_resp,
        scalars=1,
    )
    got_resp = lax.ppermute(send_resp, "xh", swap)
    (line,) = call(
        line_kernel,
        [((CHIPS, 2 * PACKED, 128), BF16)],
        sample_parts,
        keep_resp,
        got_resp,
    )
    d_key_up, d_value_up = call(
        weights_kernel,
        [((PAGE, LOCAL * DN), F32), ((PAGE, LOCAL * DV), F32)],
        sample_parts,
        flops=1_000_000_000,
    )
    lines = spread(line, ("xh", "z"))
    d_prompt, d_prompt_rope, d_resp, d_resp_rope_t = call(
        last_kernel,
        [
            ((PAGE, DC), F32),
            ((PAGE, DR), F32),
            ((RESP, DC), F32),
            ((DR, RESP), F32),
        ],
        lines,
    )
    return (
        d_q_nope,
        d_q_rope,
        d_key_up,
        d_value_up,
        d_prompt,
        jnp.transpose(d_prompt_rope),
        d_resp,
        d_resp_rope_t,
    )


def solution(mesh):
    fine = Mesh(mesh.devices.reshape(2, 8, 2, 8, 2), SAMPLE + HEAD)
    return jax.shard_map(
        body,
        mesh=fine,
        in_specs=(
            P(SAMPLE, HEAD),
            P(SAMPLE, HEAD),
            P(SAMPLE, None),
            P(None, SAMPLE),
            P(SAMPLE, None),
            P(None, SAMPLE),
            P(None, HEAD),
            P(None, HEAD),
            P(SAMPLE, HEAD),
            P(SAMPLE),
        ),
        out_specs=(
            P(SAMPLE, HEAD),
            P(SAMPLE, HEAD),
            P(SAMPLE, HEAD),
            P(SAMPLE, HEAD),
            P(SAMPLE, None),
            P(None, SAMPLE),
            P(SAMPLE, None),
            P(None, SAMPLE),
        ),
        check_vma=False,
    )
```

```python
import functools

import jax
import jax.numpy as jnp
from jax import lax
from jax.experimental import pallas as pl
from jax.experimental.pallas import tpu as pltpu
from jax.sharding import Mesh, PartitionSpec as P

DC = 512
DR = 64
DN = 128
DV = 128
RESP = 128
PAGE = 16
LOCAL = 4
ROWS = LOCAL * RESP
EXT = 640
KEY = DC + DR
CHIPS = 16
HALF = CHIPS * PAGE
KEYS = 2 * HALF + RESP
ROPE_AT = (2 * LOCAL + DC // 128) * PAGE
WIDE = ROPE_AT + 8
PACKED = DC // 128 * PAGE + 8
OWNERS = [(b & 1) + 2 * (3, 0, 1, 2)[b >> 1] for b in range(RESP // PAGE)]
ORDER = [2 * (3 * k % 8) + xh for xh in range(2) for k in range(8)]
SCALE = (DN + DR) ** (-0.5)
F32 = jnp.float32
BF16 = jnp.bfloat16
SAMPLE = ("xl", "y", "c")
HEAD = ("z", "xh")
PARAMS = pltpu.CompilerParams(vmem_limit_bytes=40 * 1024 * 1024)


def dot(a, b, ca, cb):
    return lax.dot_general(a, b, (((ca,), (cb,)), ((), ())), preferred_element_type=F32)


def columns(part, width):
    return slice(part * width, (part + 1) * width)


def with_rope(latent, rope):
    pad = jnp.zeros((latent.shape[0], EXT - DC - DR), BF16)
    return jnp.concatenate([latent, rope, pad], axis=1)


def pages_kernel(latent_far, rope_far, out, latent, rope, done):
    first = pltpu.make_async_copy(latent_far, latent, done.at[0])
    second = pltpu.make_async_copy(rope_far, rope, done.at[1])
    first.start()
    second.start()
    first.wait()
    second.wait()
    rows = rope[...].astype(F32)
    rows = jnp.concatenate([rows[0:8], rows[8:16]], axis=1).astype(BF16)
    for k in range(CHIPS):
        for part in range(DC // 128):
            out[k, columns(part, PAGE), :] = latent[:, columns(part, 128)]
        out[k, DC // 128 * PAGE : PACKED, :] = rows


def unpack(pages, keys):
    for part in range(DC // 128):
        block = pages[:, columns(part, PAGE), :]
        keys[:, columns(part, 128)] = block.reshape(HALF, 128)
    rope = pages[:, DC // 128 * PAGE : PACKED, :].astype(F32)
    rope = jnp.concatenate([rope[:, :, 0:DR], rope[:, :, DR : 2 * DR]], axis=1)
    rope = jnp.concatenate([rope, jnp.zeros_like(rope)], axis=2)
    keys[:, DC:EXT] = rope.reshape(HALF, EXT - DC).astype(BF16)


def query_kernel(
    where,
    q_nope,
    q_rope,
    grad,
    w_key,
    w_value,
    resp_latent,
    resp_rope_t,
    query,
    d_out,
    masked_out,
    resp_keys,
):
    length = where[0]
    rope = jnp.transpose(resp_rope_t[...].astype(F32)).astype(BF16)
    resp_keys[...] = with_rope(resp_latent[...], rope)
    live = lax.broadcasted_iota(jnp.int32, (RESP, LOCAL * DV), 0) < length
    masked = jnp.where(live, grad[...].astype(F32), 0.0).astype(BF16)
    masked_out[...] = masked
    for h in range(LOCAL):
        rows = columns(h, RESP)
        latent = dot(q_nope[:, columns(h, DN)], w_key[:, columns(h, DN)], 1, 1)
        query[rows, :] = with_rope(latent.astype(BF16), q_rope[:, columns(h, DR)])
        d_out[rows, :] = dot(masked[:, columns(h, DV)], w_value[:, columns(h, DV)], 1, 1).astype(
            BF16
        )


def first_scores_kernel(where, query, d_out, own, resp_keys, scores, d_attention, own_keys):
    length = where[0]
    unpack(own, own_keys)
    pages = own_keys[...]
    resp = resp_keys[...]
    scores[0:HALF, :] = dot(pages, query[...], 1, 1) * SCALE
    token = lax.broadcasted_iota(jnp.int32, (RESP, ROWS), 1) % RESP
    key_at = lax.broadcasted_iota(jnp.int32, (RESP, ROWS), 0)
    allowed = (key_at <= token) & (key_at < length)
    own_scores = dot(resp, query[...], 1, 1) * SCALE
    scores[HALF : HALF + RESP, :] = jnp.where(allowed, own_scores, -1e30)
    d_attention[0:HALF, :] = dot(pages[:, 0:DC], d_out[...], 1, 1)
    d_attention[HALF : HALF + RESP, :] = dot(resp[:, 0:DC], d_out[...], 1, 1)


def attention_kernel(
    where,
    q_nope,
    masked,
    query,
    d_out,
    own,
    other,
    resp_keys,
    first_scores,
    first_d_attention,
    attention_out,
    d_scores_out,
    d_query,
    out_latent,
    send,
    keys,
):
    keys[0:HALF, :] = own[...]
    unpack(other, keys.at[HALF : 2 * HALF])
    keys[2 * HALF : KEYS, :] = resp_keys[...]
    other_rows = keys[HALF : 2 * HALF, :]
    other_scores = dot(other_rows, query[...], 1, 1) * SCALE
    scores = jnp.concatenate(
        [first_scores[0:HALF], other_scores, first_scores[HALF : HALF + RESP]], axis=0
    )
    highest = jnp.max(scores, axis=0, keepdims=True)
    exponent = jnp.exp(scores - highest)
    attention = exponent * (1.0 / jnp.sum(exponent, axis=0, keepdims=True))
    attention_b = attention.astype(BF16)
    attention_out[...] = attention_b
    d_attention = jnp.concatenate(
        [
            first_d_attention[0:HALF],
            dot(other_rows[:, 0:DC], d_out[...], 1, 1),
            first_d_attention[HALF : HALF + RESP],
        ],
        axis=0,
    )
    row_delta = jnp.sum(attention * d_attention, axis=0, keepdims=True)
    d_scores = (SCALE * attention * (d_attention - row_delta)).astype(BF16)
    d_scores_out[...] = d_scores
    d_query[...] = dot(keys[...], d_scores, 0, 0).astype(BF16)
    out_latent[...] = dot(keys[:, 0:DC], attention_b, 0, 0).astype(BF16)
    half_grads(
        1 - where[1],
        HALF,
        q_nope,
        masked,
        query,
        d_out,
        attention_out,
        d_scores_out,
        d_query,
        out_latent,
        send,
    )


def half_grads(parity, first_key, q_nope, masked, query, d_out, attention, d_scores, d_query, out_latent, out):
    starts = [pl.multiple_of((2 * k + parity) * PAGE, PAGE) for k in range(CHIPS)]
    d_q = jnp.concatenate([d_query[pl.ds(start, PAGE), :] for start in starts], axis=0)
    values = jnp.concatenate([out_latent[pl.ds(start, PAGE), :] for start in starts], axis=0)
    blocks = []
    for h in range(LOCAL):
        blocks.append(dot(d_q[:, columns(h, RESP)], q_nope[:, columns(h, DN)], 1, 0))
    for h in range(LOCAL):
        blocks.append(dot(values[:, columns(h, RESP)], masked[:, columns(h, DV)], 1, 0))
    rows = slice(first_key, first_key + HALF)
    key_grad = dot(d_scores[rows, :], query[...], 1, 0)
    latent_part = key_grad[:, 0:DC] + dot(attention[rows, :], d_out[...], 1, 0)
    blocks += [latent_part[:, columns(part, 128)] for part in range(DC // 128)]
    for at, block in enumerate(blocks):
        out[:, columns(at, PAGE), :] = block.astype(BF16).reshape(CHIPS, PAGE, 128)
    rope = key_grad[:, DC : DC + DR].reshape(CHIPS, PAGE, DR)
    rope = jnp.concatenate([rope[:, 0:8], rope[:, 8:16]], axis=2)
    out[:, ROPE_AT:WIDE, :] = rope.astype(BF16)


def keep_kernel(
    where,
    q_nope,
    masked,
    query,
    d_out,
    attention,
    d_scores,
    d_query,
    out_latent,
    keep,
    keep_resp,
    send_resp,
):
    half_grads(where[1], 0, q_nope, masked, query, d_out, attention, d_scores, d_query, out_latent, keep)
    own_grad = dot(d_scores[2 * HALF : KEYS, :], query[...], 1, 0)
    own_grad_v = dot(attention[2 * HALF : KEYS, :], d_out[...], 1, 0)
    latent = (own_grad[:, 0:DC] + own_grad_v).reshape(RESP // PAGE, PAGE, DC)
    rope = own_grad[:, DC:KEY].reshape(RESP // PAGE, PAGE, DR)
    packed = jnp.concatenate(
        [latent[:, :, columns(part, 128)] for part in range(DC // 128)]
        + [jnp.concatenate([rope[:, 0:8], rope[:, 8:16]], axis=2)],
        axis=1,
    ).astype(BF16)
    place = where[2]
    for g in range(RESP // PAGE // 2):
        low, high = packed[g], packed[RESP // PAGE // 2 + g]
        keep_resp[g] = jnp.where(place == 0, low, high)
        send_resp[g] = jnp.where(place == 0, high, low)


def query_grad_kernel(d_query, w_key, d_q_nope, d_q_rope):
    for h in range(LOCAL):
        d_q = d_query[0:DC, columns(h, RESP)]
        d_q_nope[:, columns(h, DN)] = dot(d_q, w_key[:, columns(h, DN)], 0, 0).astype(BF16)
    d_rope = jnp.concatenate(
        [
            jnp.transpose(d_query[DC : DC + DR, columns(h, RESP)].astype(F32)) for h in range(LOCAL)
        ],
        axis=1,
    )
    d_q_rope[...] = d_rope.astype(BF16)


def halve_kernel(bit, where, kept, received, keep, send):
    half = keep.shape[0]
    place = where[bit]
    mine = pl.ds(place * half, half)
    theirs = pl.ds((1 - place) * half, half)
    keep[...] = (kept[mine].astype(F32) + received[mine].astype(F32)).astype(BF16)
    send[...] = (kept[theirs].astype(F32) + received[theirs].astype(F32)).astype(BF16)


def add_blocks(parts, rows):
    total = parts[0, rows, :].astype(F32)
    for k in range(1, CHIPS):
        total = total + parts[k, rows, :].astype(F32)
    return total


def line_kernel(sample_parts, kept, received, out):
    page = add_blocks(sample_parts, slice(2 * LOCAL * PAGE, WIDE))
    rows = kept[0].astype(F32) + received[0].astype(F32)
    line = jnp.concatenate([rows, page], axis=0).astype(BF16)
    for g in range(CHIPS):
        out[g] = line


def weights_kernel(sample_parts, d_key_up, d_value_up):
    total = add_blocks(sample_parts, slice(0, 2 * LOCAL * PAGE))
    for h in range(LOCAL):
        d_key_up[:, columns(h, DN)] = total[columns(h, PAGE)]
        d_value_up[:, columns(h, DV)] = total[columns(LOCAL + h, PAGE)]


def unpacked(block):
    latent = [block[columns(part, PAGE)] for part in range(DC // 128)]
    rope = block[DC // 128 * PAGE : PACKED]
    return (
        jnp.concatenate(latent, axis=1),
        jnp.concatenate([rope[:, 0:DR], rope[:, DR : 2 * DR]], axis=0),
    )


def last_kernel(parts, d_prompt, d_prompt_rope, d_resp, d_resp_rope_t):
    latent, rope = unpacked(add_blocks(parts, slice(PACKED, 2 * PACKED)))
    d_prompt[...] = latent
    d_prompt_rope[...] = rope
    ropes = []
    for at, g in enumerate(OWNERS):
        low, high = ORDER.index(g), ORDER.index(g + 8)
        block = parts[low, 0:PACKED, :].astype(F32) + parts[high, 0:PACKED, :].astype(F32)
        latent, rope = unpacked(block)
        d_resp[columns(at, PAGE), :] = latent
        ropes.append(rope)
    d_resp_rope_t[...] = jnp.transpose(jnp.concatenate(ropes, axis=0))


def call(kernel, outs, *args, scratch=(), scalars=0, flops=0, far=False):
    vmem = pl.BlockSpec(memory_space=pltpu.VMEM)
    smem = pl.BlockSpec(memory_space=pltpu.SMEM)
    return pl.pallas_call(
        kernel,
        out_shape=[jax.ShapeDtypeStruct(shape, kind) for shape, kind in outs],
        in_specs=[smem] * scalars + [pl.BlockSpec(memory_space=pltpu.HBM) if far else vmem] * (len(args) - scalars),
        out_specs=[vmem] * len(outs),
        scratch_shapes=list(scratch),
        compiler_params=PARAMS,
        cost_estimate=pl.CostEstimate(flops=flops, bytes_accessed=0, transcendentals=0),
    )(*args)


def spread(parts, axes):
    return lax.all_to_all(parts, axes, 0, 0, tiled=True)


def body(
    q_nope,
    q_rope,
    resp_latent,
    resp_rope_t,
    prompt_latent,
    prompt_rope_t,
    w_key_up,
    w_value_up,
    grad_out,
    lengths,
):
    swap = [(0, 1), (1, 0)]
    (pages,) = call(
        pages_kernel,
        [((CHIPS, PACKED, 128), BF16)],
        pltpu.with_memory_space_constraint(prompt_latent, pltpu.HBM),
        pltpu.with_memory_space_constraint(jnp.transpose(prompt_rope_t), pltpu.HBM),
        far=True,
        scratch=[
            pltpu.VMEM((PAGE, DC), BF16),
            pltpu.VMEM((PAGE, DR), BF16),
            pltpu.SemaphoreType.DMA((2,)),
        ],
    )
    own = spread(pages, ("xl", "y"))
    z = lax.axis_index("z")
    where = jnp.stack(
        [lengths[0], lax.axis_index("c"), (z + 1) >> 1 & 1, 1 - (z & 1), lax.axis_index("xh")]
    )
    query, d_out, masked, resp_keys = call(
        query_kernel,
        [
            ((ROWS, EXT), BF16),
            ((ROWS, DC), BF16),
            ((RESP, LOCAL * DV), BF16),
            ((RESP, EXT), BF16),
        ],
        where,
        q_nope,
        q_rope,
        grad_out,
        w_key_up,
        w_value_up,
        resp_latent,
        resp_rope_t,
        scalars=1,
        flops=4_000_000_000,
    )
    own, query = lax.optimization_barrier((own, query))
    other = lax.ppermute(own, "c", swap)
    first_scores, first_d_attention, own_keys = call(
        first_scores_kernel,
        [((HALF + RESP, ROWS), F32)] * 2 + [((HALF, EXT), BF16)],
        where,
        query,
        d_out,
        own,
        resp_keys,
        scalars=1,
        flops=2_000_000_000,
    )
    attention, d_scores, d_query, out_latent, send = call(
        attention_kernel,
        [
            ((KEYS, ROWS), BF16),
            ((KEYS, ROWS), BF16),
            ((EXT, ROWS), BF16),
            ((DC, ROWS), BF16),
            ((CHIPS, WIDE, 128), BF16),
        ],
        where,
        q_nope,
        masked,
        query,
        d_out,
        own_keys,
        other,
        resp_keys,
        first_scores,
        first_d_attention,
        scalars=1,
        flops=4_000_000_000,
        scratch=[pltpu.VMEM((KEYS, EXT), BF16)],
    )
    keep, keep_resp, send_resp = call(
        keep_kernel,
        [
            ((CHIPS, WIDE, 128), BF16),
            ((RESP // PAGE // 2, PACKED, 128), BF16),
            ((RESP // PAGE // 2, PACKED, 128), BF16),
        ],
        where,
        q_nope,
        masked,
        query,
        d_out,
        attention,
        d_scores,
        d_query,
        out_latent,
        scalars=1,
        flops=2_000_000_000,
    )
    got_resp = lax.ppermute(send_resp, "z", [(i, i ^ 1) for i in range(8)])
    chip_sum = keep + lax.ppermute(send, "c", swap)
    sample_parts = spread(chip_sum, ("xl", "y"))
    d_q_nope, d_q_rope = call(
        query_grad_kernel,
        [((RESP, LOCAL * DN), BF16), ((RESP, LOCAL * DR), BF16)],
        d_query,
        w_key_up,
        flops=1_000_000_000,
    )
    keep_resp, send_resp = call(
        functools.partial(halve_kernel, 3),
        [((2, PACKED, 128), BF16)] * 2,
        where,
        keep_resp,
        got_resp,
        scalars=1,
    )
    got_resp = lax.ppermute(send_resp, "z", [(i, (i + 2 * (i & 1) - 1) % 8) for i in range(8)])
    keep_resp, send_resp = call(
        functools.partial(halve_kernel, 4),
        [((1, PACKED, 128), BF16)] * 2,
        where,
        keep_resp,
        got_resp,
        scalars=1,
    )
    got_resp = lax.ppermute(send_resp, "xh", swap)
    (line,) = call(
        line_kernel,
        [((CHIPS, 2 * PACKED, 128), BF16)],
        sample_parts,
        keep_resp,
        got_resp,
    )
    d_key_up, d_value_up = call(
        weights_kernel,
        [((PAGE, LOCAL * DN), F32), ((PAGE, LOCAL * DV), F32)],
        sample_parts,
        flops=1_000_000_000,
    )
    lines = lax.all_to_all(
        line, HEAD, 0, 0, axis_index_groups=[ORDER], tiled=True
    )
    d_prompt, d_prompt_rope, d_resp, d_resp_rope_t = call(
        last_kernel,
        [
            ((PAGE, DC), F32),
            ((PAGE, DR), F32),
            ((RESP, DC), F32),
            ((DR, RESP), F32),
        ],
        lines,
    )
    return (
        d_q_nope,
        d_q_rope,
        d_key_up,
        d_value_up,
        d_prompt,
        jnp.transpose(d_prompt_rope),
        d_resp,
        d_resp_rope_t,
    )


def solution(mesh):
    fine = Mesh(mesh.devices.reshape(2, 8, 2, 8, 2), SAMPLE + HEAD)
    return jax.shard_map(
        body,
        mesh=fine,
        in_specs=(
            P(SAMPLE, HEAD),
            P(SAMPLE, HEAD),
            P(SAMPLE, None),
            P(None, SAMPLE),
            P(SAMPLE, None),
            P(None, SAMPLE),
            P(None, HEAD),
            P(None, HEAD),
            P(SAMPLE, HEAD),
            P(SAMPLE),
        ),
        out_specs=(
            P(SAMPLE, HEAD),
            P(SAMPLE, HEAD),
            P(SAMPLE, HEAD),
            P(SAMPLE, HEAD),
            P(SAMPLE, None),
            P(None, SAMPLE),
            P(SAMPLE, None),
            P(None, SAMPLE),
        ),
        check_vma=False,
    )
```

```python
import functools

import jax
import jax.numpy as jnp
from jax import lax
from jax.experimental import pallas as pl
from jax.experimental.pallas import tpu as pltpu
from jax.sharding import Mesh, PartitionSpec as P

DC = 512
DR = 64
DN = 128
DV = 128
RESP = 128
PAGE = 16
LOCAL = 4
ROWS = LOCAL * RESP
EXT = 640
KEY = DC + DR
CHIPS = 16
HALF = CHIPS * PAGE
KEYS = 2 * HALF + RESP
ROPE_AT = (2 * LOCAL + DC // 128) * PAGE
WIDE = ROPE_AT + 8
PACKED = DC // 128 * PAGE + 8
OWNERS = [(b & 1) + 2 * (3, 0, 1, 2)[b >> 1] for b in range(RESP // PAGE)]
ORDER = [2 * (3 * k % 8) + xh for xh in range(2) for k in range(8)]
SCALE = (DN + DR) ** (-0.5)
F32 = jnp.float32
BF16 = jnp.bfloat16
SAMPLE = ("xl", "y", "c")
HEAD = ("z", "xh")
PARAMS = pltpu.CompilerParams(vmem_limit_bytes=40 * 1024 * 1024)


def dot(a, b, ca, cb):
    return lax.dot_general(a, b, (((ca,), (cb,)), ((), ())), preferred_element_type=F32)


def columns(part, width):
    return slice(part * width, (part + 1) * width)


def with_rope(latent, rope):
    pad = jnp.zeros((latent.shape[0], EXT - DC - DR), BF16)
    return jnp.concatenate([latent, rope, pad], axis=1)


def pages_kernel(latent_far, rope_far, out, latent, rope, done):
    first = pltpu.make_async_copy(latent_far, latent, done.at[0])
    second = pltpu.make_async_copy(rope_far, rope, done.at[1])
    first.start()
    second.start()
    first.wait()
    second.wait()
    rows = rope[...].astype(F32)
    rows = jnp.concatenate([rows[0:8], rows[8:16]], axis=1).astype(BF16)
    for k in range(CHIPS):
        for part in range(DC // 128):
            out[k, columns(part, PAGE), :] = latent[:, columns(part, 128)]
        out[k, DC // 128 * PAGE : PACKED, :] = rows


def unpack(pages, keys):
    for part in range(DC // 128):
        block = pages[:, columns(part, PAGE), :]
        keys[:, columns(part, 128)] = block.reshape(HALF, 128)
    rope = pages[:, DC // 128 * PAGE : PACKED, :].astype(F32)
    rope = jnp.concatenate([rope[:, :, 0:DR], rope[:, :, DR : 2 * DR]], axis=1)
    rope = jnp.concatenate([rope, jnp.zeros_like(rope)], axis=2)
    keys[:, DC:EXT] = rope.reshape(HALF, EXT - DC).astype(BF16)


def query_kernel(
    where,
    q_nope,
    q_rope,
    grad,
    w_key,
    w_value,
    resp_latent,
    resp_rope_t,
    query,
    d_out,
    masked_out,
    resp_keys,
):
    length = where[0]
    rope = jnp.transpose(resp_rope_t[...].astype(F32)).astype(BF16)
    resp_keys[...] = with_rope(resp_latent[...], rope)
    live = lax.broadcasted_iota(jnp.int32, (RESP, LOCAL * DV), 0) < length
    masked = jnp.where(live, grad[...].astype(F32), 0.0).astype(BF16)
    masked_out[...] = masked
    for h in range(LOCAL):
        rows = columns(h, RESP)
        latent = dot(q_nope[:, columns(h, DN)], w_key[:, columns(h, DN)], 1, 1)
        query[rows, :] = with_rope(latent.astype(BF16), q_rope[:, columns(h, DR)])
        d_out[rows, :] = dot(masked[:, columns(h, DV)], w_value[:, columns(h, DV)], 1, 1).astype(
            BF16
        )


def first_scores_kernel(where, query, d_out, own, resp_keys, scores, d_attention, own_keys):
    length = where[0]
    unpack(own, own_keys)
    pages = own_keys[...]
    resp = resp_keys[...]
    scores[0:HALF, :] = dot(pages, query[...], 1, 1) * SCALE
    token = lax.broadcasted_iota(jnp.int32, (RESP, ROWS), 1) % RESP
    key_at = lax.broadcasted_iota(jnp.int32, (RESP, ROWS), 0)
    allowed = (key_at <= token) & (key_at < length)
    own_scores = dot(resp, query[...], 1, 1) * SCALE
    scores[HALF : HALF + RESP, :] = jnp.where(allowed, own_scores, -1e30)
    d_attention[0:HALF, :] = dot(pages[:, 0:DC], d_out[...], 1, 1)
    d_attention[HALF : HALF + RESP, :] = dot(resp[:, 0:DC], d_out[...], 1, 1)


def attention_kernel(
    q_nope,
    masked,
    query,
    d_out,
    own,
    other,
    resp_keys,
    first_scores,
    first_d_attention,
    attention_out,
    d_scores_out,
    d_query,
    out_latent,
    send,
    keys,
):
    keys[0:HALF, :] = own[...]
    unpack(other, keys.at[HALF : 2 * HALF])
    keys[2 * HALF : KEYS, :] = resp_keys[...]
    other_rows = keys[HALF : 2 * HALF, :]
    other_scores = dot(other_rows, query[...], 1, 1) * SCALE
    scores = jnp.concatenate(
        [first_scores[0:HALF], other_scores, first_scores[HALF : HALF + RESP]], axis=0
    )
    highest = jnp.max(scores, axis=0, keepdims=True)
    exponent = jnp.exp(scores - highest)
    attention = exponent * (1.0 / jnp.sum(exponent, axis=0, keepdims=True))
    attention_b = attention.astype(BF16)
    attention_out[...] = attention_b
    d_attention = jnp.concatenate(
        [
            first_d_attention[0:HALF],
            dot(other_rows[:, 0:DC], d_out[...], 1, 1),
            first_d_attention[HALF : HALF + RESP],
        ],
        axis=0,
    )
    row_delta = jnp.sum(attention * d_attention, axis=0, keepdims=True)
    d_scores = (SCALE * attention * (d_attention - row_delta)).astype(BF16)
    d_scores_out[...] = d_scores
    d_query[...] = dot(keys[...], d_scores, 0, 0).astype(BF16)
    out_latent[...] = dot(keys[:, 0:DC], attention_b, 0, 0).astype(BF16)
    half_grads(
        1 - lax.axis_index("c"),
        HALF,
        q_nope,
        masked,
        query,
        d_out,
        attention_out,
        d_scores_out,
        d_query,
        out_latent,
        send,
    )


def half_grads(parity, first_key, q_nope, masked, query, d_out, attention, d_scores, d_query, out_latent, out):
    starts = [pl.multiple_of((2 * k + parity) * PAGE, PAGE) for k in range(CHIPS)]
    d_q = jnp.concatenate([d_query[pl.ds(start, PAGE), :] for start in starts], axis=0)
    values = jnp.concatenate([out_latent[pl.ds(start, PAGE), :] for start in starts], axis=0)
    blocks = []
    for h in range(LOCAL):
        blocks.append(dot(d_q[:, columns(h, RESP)], q_nope[:, columns(h, DN)], 1, 0))
    for h in range(LOCAL):
        blocks.append(dot(values[:, columns(h, RESP)], masked[:, columns(h, DV)], 1, 0))
    rows = slice(first_key, first_key + HALF)
    key_grad = dot(d_scores[rows, :], query[...], 1, 0)
    latent_part = key_grad[:, 0:DC] + dot(attention[rows, :], d_out[...], 1, 0)
    blocks += [latent_part[:, columns(part, 128)] for part in range(DC // 128)]
    for at, block in enumerate(blocks):
        out[:, columns(at, PAGE), :] = block.astype(BF16).reshape(CHIPS, PAGE, 128)
    rope = key_grad[:, DC : DC + DR].reshape(CHIPS, PAGE, DR)
    rope = jnp.concatenate([rope[:, 0:8], rope[:, 8:16]], axis=2)
    out[:, ROPE_AT:WIDE, :] = rope.astype(BF16)


def keep_kernel(
    where,
    q_nope,
    masked,
    query,
    d_out,
    attention,
    d_scores,
    d_query,
    out_latent,
    keep,
    keep_resp,
    send_resp,
):
    half_grads(where[1], 0, q_nope, masked, query, d_out, attention, d_scores, d_query, out_latent, keep)
    own_grad = dot(d_scores[2 * HALF : KEYS, :], query[...], 1, 0)
    own_grad_v = dot(attention[2 * HALF : KEYS, :], d_out[...], 1, 0)
    latent = (own_grad[:, 0:DC] + own_grad_v).reshape(RESP // PAGE, PAGE, DC)
    rope = own_grad[:, DC:KEY].reshape(RESP // PAGE, PAGE, DR)
    packed = jnp.concatenate(
        [latent[:, :, columns(part, 128)] for part in range(DC // 128)]
        + [jnp.concatenate([rope[:, 0:8], rope[:, 8:16]], axis=2)],
        axis=1,
    ).astype(BF16)
    place = where[2]
    for g in range(RESP // PAGE // 2):
        low, high = packed[g], packed[RESP // PAGE // 2 + g]
        keep_resp[g] = jnp.where(place == 0, low, high)
        send_resp[g] = jnp.where(place == 0, high, low)


def query_grad_kernel(d_query, w_key, d_q_nope, d_q_rope):
    for h in range(LOCAL):
        d_q = d_query[0:DC, columns(h, RESP)]
        d_q_nope[:, columns(h, DN)] = dot(d_q, w_key[:, columns(h, DN)], 0, 0).astype(BF16)
    d_rope = jnp.concatenate(
        [
            jnp.transpose(d_query[DC : DC + DR, columns(h, RESP)].astype(F32)) for h in range(LOCAL)
        ],
        axis=1,
    )
    d_q_rope[...] = d_rope.astype(BF16)


def halve_kernel(bit, kept, received, keep, send):
    half = keep.shape[0]
    place = lax.axis_index("xh") if bit else 1 - (lax.axis_index("z") & 1)
    mine = pl.ds(place * half, half)
    theirs = pl.ds((1 - place) * half, half)
    keep[...] = (kept[mine].astype(F32) + received[mine].astype(F32)).astype(BF16)
    send[...] = (kept[theirs].astype(F32) + received[theirs].astype(F32)).astype(BF16)


def add_blocks(parts, rows):
    total = parts[0, rows, :].astype(F32)
    for k in range(1, CHIPS):
        total = total + parts[k, rows, :].astype(F32)
    return total


def line_kernel(sample_parts, kept, received, out):
    page = add_blocks(sample_parts, slice(2 * LOCAL * PAGE, WIDE))
    rows = kept[0].astype(F32) + received[0].astype(F32)
    line = jnp.concatenate([rows, page], axis=0).astype(BF16)
    for g in range(CHIPS):
        out[g] = line


def weights_kernel(sample_parts, d_key_up, d_value_up):
    total = add_blocks(sample_parts, slice(0, 2 * LOCAL * PAGE))
    for h in range(LOCAL):
        d_key_up[:, columns(h, DN)] = total[columns(h, PAGE)]
        d_value_up[:, columns(h, DV)] = total[columns(LOCAL + h, PAGE)]


def unpacked(block):
    latent = [block[columns(part, PAGE)] for part in range(DC // 128)]
    rope = block[DC // 128 * PAGE : PACKED]
    return (
        jnp.concatenate(latent, axis=1),
        jnp.concatenate([rope[:, 0:DR], rope[:, DR : 2 * DR]], axis=0),
    )


def last_kernel(parts, d_prompt, d_prompt_rope, d_resp, d_resp_rope_t):
    latent, rope = unpacked(add_blocks(parts, slice(PACKED, 2 * PACKED)))
    d_prompt[...] = latent
    d_prompt_rope[...] = rope
    ropes = []
    for at, g in enumerate(OWNERS):
        low, high = ORDER.index(g), ORDER.index(g + 8)
        block = parts[low, 0:PACKED, :].astype(F32) + parts[high, 0:PACKED, :].astype(F32)
        latent, rope = unpacked(block)
        d_resp[columns(at, PAGE), :] = latent
        ropes.append(rope)
    d_resp_rope_t[...] = jnp.transpose(jnp.concatenate(ropes, axis=0))


def call(kernel, outs, *args, scratch=(), scalars=0, flops=0, far=False):
    vmem = pl.BlockSpec(memory_space=pltpu.VMEM)
    smem = pl.BlockSpec(memory_space=pltpu.SMEM)
    return pl.pallas_call(
        kernel,
        out_shape=[jax.ShapeDtypeStruct(shape, kind) for shape, kind in outs],
        in_specs=[smem] * scalars + [pl.BlockSpec(memory_space=pltpu.HBM) if far else vmem] * (len(args) - scalars),
        out_specs=[vmem] * len(outs),
        scratch_shapes=list(scratch),
        compiler_params=PARAMS,
        cost_estimate=pl.CostEstimate(flops=flops, bytes_accessed=0, transcendentals=0),
    )(*args)


def spread(parts, axes):
    return lax.all_to_all(parts, axes, 0, 0, tiled=True)


def body(
    q_nope,
    q_rope,
    resp_latent,
    resp_rope_t,
    prompt_latent,
    prompt_rope_t,
    w_key_up,
    w_value_up,
    grad_out,
    lengths,
):
    swap = [(0, 1), (1, 0)]
    (pages,) = call(
        pages_kernel,
        [((CHIPS, PACKED, 128), BF16)],
        pltpu.with_memory_space_constraint(prompt_latent, pltpu.HBM),
        pltpu.with_memory_space_constraint(jnp.transpose(prompt_rope_t), pltpu.HBM),
        far=True,
        scratch=[
            pltpu.VMEM((PAGE, DC), BF16),
            pltpu.VMEM((PAGE, DR), BF16),
            pltpu.SemaphoreType.DMA((2,)),
        ],
    )
    own = spread(pages, ("xl", "y"))
    z = lax.axis_index("z")
    where = jnp.stack(
        [lengths[0], lax.axis_index("c"), (z + 1) >> 1 & 1, 1 - (z & 1), lax.axis_index("xh")]
    )
    query, d_out, masked, resp_keys = call(
        query_kernel,
        [
            ((ROWS, EXT), BF16),
            ((ROWS, DC), BF16),
            ((RESP, LOCAL * DV), BF16),
            ((RESP, EXT), BF16),
        ],
        where,
        q_nope,
        q_rope,
        grad_out,
        w_key_up,
        w_value_up,
        resp_latent,
        resp_rope_t,
        scalars=1,
        flops=4_000_000_000,
    )
    own, query = lax.optimization_barrier((own, query))
    other = lax.ppermute(own, "c", swap)
    first_scores, first_d_attention, own_keys = call(
        first_scores_kernel,
        [((HALF + RESP, ROWS), F32)] * 2 + [((HALF, EXT), BF16)],
        where,
        query,
        d_out,
        own,
        resp_keys,
        scalars=1,
        flops=2_000_000_000,
    )
    attention, d_scores, d_query, out_latent, send = call(
        attention_kernel,
        [
            ((KEYS, ROWS), BF16),
            ((KEYS, ROWS), BF16),
            ((EXT, ROWS), BF16),
            ((DC, ROWS), BF16),
            ((CHIPS, WIDE, 128), BF16),
        ],
        q_nope,
        masked,
        query,
        d_out,
        own_keys,
        other,
        resp_keys,
        first_scores,
        first_d_attention,
        flops=4_000_000_000,
        scratch=[pltpu.VMEM((KEYS, EXT), BF16)],
    )
    keep, keep_resp, send_resp = call(
        keep_kernel,
        [
            ((CHIPS, WIDE, 128), BF16),
            ((RESP // PAGE // 2, PACKED, 128), BF16),
            ((RESP // PAGE // 2, PACKED, 128), BF16),
        ],
        where,
        q_nope,
        masked,
        query,
        d_out,
        attention,
        d_scores,
        d_query,
        out_latent,
        scalars=1,
        flops=2_000_000_000,
    )
    got_resp = lax.ppermute(send_resp, "z", [(i, i ^ 1) for i in range(8)])
    chip_sum = keep + lax.ppermute(send, "c", swap)
    sample_parts = spread(chip_sum, ("xl", "y"))
    d_q_nope, d_q_rope = call(
        query_grad_kernel,
        [((RESP, LOCAL * DN), BF16), ((RESP, LOCAL * DR), BF16)],
        d_query,
        w_key_up,
        flops=1_000_000_000,
    )
    keep_resp, send_resp = call(
        functools.partial(halve_kernel, 0),
        [((2, PACKED, 128), BF16)] * 2,
        keep_resp,
        got_resp,
    )
    got_resp = lax.ppermute(send_resp, "z", [(i, (i + 2 * (i & 1) - 1) % 8) for i in range(8)])
    keep_resp, send_resp = call(
        functools.partial(halve_kernel, 1),
        [((1, PACKED, 128), BF16)] * 2,
        keep_resp,
        got_resp,
    )
    got_resp = lax.ppermute(send_resp, "xh", swap)
    (line,) = call(
        line_kernel,
        [((CHIPS, 2 * PACKED, 128), BF16)],
        sample_parts,
        keep_resp,
        got_resp,
    )
    d_key_up, d_value_up = call(
        weights_kernel,
        [((PAGE, LOCAL * DN), F32), ((PAGE, LOCAL * DV), F32)],
        sample_parts,
        flops=1_000_000_000,
    )
    lines = lax.all_to_all(
        line, HEAD, 0, 0, axis_index_groups=[ORDER], tiled=True
    )
    d_prompt, d_prompt_rope, d_resp, d_resp_rope_t = call(
        last_kernel,
        [
            ((PAGE, DC), F32),
            ((PAGE, DR), F32),
            ((RESP, DC), F32),
            ((DR, RESP), F32),
        ],
        lines,
    )
    return (
        d_q_nope,
        d_q_rope,
        d_key_up,
        d_value_up,
        d_prompt,
        jnp.transpose(d_prompt_rope),
        d_resp,
        d_resp_rope_t,
    )


def solution(mesh):
    fine = Mesh(mesh.devices.reshape(2, 8, 2, 8, 2), SAMPLE + HEAD)
    return jax.shard_map(
        body,
        mesh=fine,
        in_specs=(
            P(SAMPLE, HEAD),
            P(SAMPLE, HEAD),
            P(SAMPLE, None),
            P(None, SAMPLE),
            P(SAMPLE, None),
            P(None, SAMPLE),
            P(None, HEAD),
            P(None, HEAD),
            P(SAMPLE, HEAD),
            P(SAMPLE),
        ),
        out_specs=(
            P(SAMPLE, HEAD),
            P(SAMPLE, HEAD),
            P(SAMPLE, HEAD),
            P(SAMPLE, HEAD),
            P(SAMPLE, None),
            P(None, SAMPLE),
            P(SAMPLE, None),
            P(None, SAMPLE),
        ),
        check_vma=False,
    )
```
